32 devices in a mesh: users: 16 (over z, y, x), cand: 2 (over core).
Axes of the slice: x: 2, y: 2, z: 4, core: 2. Of those that a mesh axis runs over, the one named last changes fastest.
Arguments:
- candidate_rows: bfloat16 [2048, 1024], P(('users', 'cand')), may hold values from -6 to 6
- weight_in: bfloat16 [2, 1024, 8, 512], P(None, None, 'cand'), may hold values from -0.1875 to 0.1875
- weight_out: bfloat16 [2, 8, 128, 1024], P(None, 'cand'), may hold values from -0.1875 to 0.1875
- history_cache: bfloat16 [2, 2, 2048, 8, 128], P(None, None, 'users', 'cand'), may hold values from -6 to 6
- block_user: int32 [16], replicated, may hold values from 0 to 3, as said below
- block_offset: int32 [16], replicated, may hold values from 0 to 7, as said below
- history_length: int32 [4], replicated, may hold values from 1 to 1024, as said below
- candidate_count: int32 [4], replicated, may hold values from 1 to 1024, as said below
Outputs:
- scored_rows: bfloat16 [2048, 1024], P(('users', 'cand'))
The draws below stay inside these ranges and needn't reach their ends.
Inputs may be any that keep to these rules, and one draw needn't show every extreme that they name: `block_user`: every one of the 4 users owns at least one block; the blocks of one user may stand anywhere; exactly one user owns 16 / 2 blocks, every other user fewer. `block_offset`: the blocks of a user that owns b blocks carry the offsets 0 to b - 1, each once. `history_length`: a user that owns b blocks has more than (b - 1) * 128 and at most b * 128 history rows. `candidate_count`: the counts sum to 2048; the rows of one user are consecutive, users in increasing order.
All inputs are finite; a program needn't handle non-finite values.
Results may differ from the reference program's by a relative error of at most 0.027.
Values may be sent and summed in bfloat16 or wider, within the bound.
No kernel may reach another device: no remote copies, remote signals or barrier semaphores. Data moves between devices by JAX's collectives and lax.ppermute only.
A program may use at most 64 MiB of HBM per device.

```python
import math
import jax
import jax.numpy as jnp
from jax import lax

D = 1024
HEADS = 8
DH = 128
LAYERS = 2
BLOCK = 128
NU = 4
NBLK = 16
NROWS = 2048
CAND = 2048
N_CAND = 2


def split_points(key, total, pieces):
    cut_points = jnp.sort(jax.random.permutation(key, total - 1)[:pieces - 1].astype(jnp.int32) + 1)
    boundaries = jnp.concatenate([jnp.zeros((1,), jnp.int32), cut_points, jnp.full((1,), total, jnp.int32)])
    return boundaries


def heavy_split(key, total, pieces):
    heavy_key, rest_key = jax.random.split(key, 2)
    heavy_size = total // 2
    heavy_user = jax.random.randint(heavy_key, (), 0, pieces).astype(jnp.int32)
    rest_bounds = split_points(rest_key, total - heavy_size, pieces - 1)
    others = rest_bounds[1:] - rest_bounds[:-1]
    users_all = jnp.arange(pieces, dtype=jnp.int32)
    below = others[jnp.clip(users_all, 0, pieces - 2)]
    above = others[jnp.clip(users_all - 1, 0, pieces - 2)]
    sizes = jnp.where(users_all < heavy_user, below, jnp.where(users_all == heavy_user, heavy_size, above)).astype(jnp.int32)
    return (sizes, heavy_user)


def history_plan(key):
    folded = jax.random.fold_in(key, 7)
    cut_key, order_key, tail_key = jax.random.split(folded, 3)
    per_user, heavy_user = heavy_split(cut_key, NBLK, NU)
    boundaries = jnp.concatenate([jnp.zeros((1,), jnp.int32), jnp.cumsum(per_user).astype(jnp.int32)])
    cut_points = boundaries[1:-1]
    sorted_ids = jnp.arange(NBLK, dtype=jnp.int32)
    owner_sorted = jnp.sum((sorted_ids[:, None] >= cut_points[None, :]).astype(jnp.int32), axis=1)
    offset_sorted = sorted_ids - boundaries[owner_sorted]
    shuffle = jax.random.permutation(order_key, NBLK)
    owners = owner_sorted[shuffle]
    offsets = offset_sorted[shuffle]
    tail_rows = jax.random.randint(tail_key, (NU,), 1, BLOCK + 1).astype(jnp.int32)
    tail_rows = jnp.where(jnp.arange(NU, dtype=jnp.int32) == heavy_user, BLOCK, tail_rows)
    lengths = (per_user - 1) * BLOCK + tail_rows
    return (owners, offsets, lengths)


def draw_block_user(key, part):
    return history_plan(key)[0]


def draw_block_offset(key, part):
    return history_plan(key)[1]


def draw_history_length(key, part):
    return history_plan(key)[2]


def draw_candidate_count(key, part):
    folded = jax.random.fold_in(key, 23)
    sizes, heavy_user = heavy_split(folded, CAND, NU)
    return sizes


def shard_levels(stream_key, extent, shards, least, top_value):
    gain = 1.0
    for axis_at, parts in shards:
        heights = jax.random.uniform(jax.random.fold_in(jax.random.fold_in(stream_key, 6), axis_at), (parts,), jnp.float32, least / len(shards), top_value / len(shards))
        gain = gain * jnp.repeat(jnp.exp(heights), extent[axis_at] // parts).reshape((-1,) + (1,) * (len(extent) - 1 - axis_at))
    return gain


def gaussian(key, dims, spread, limit, shards=(), kind=jnp.bfloat16):
    level = shard_levels(key, dims, shards, -0.22, 0.18) if shards else 1.0
    array = jax.random.normal(key, dims, jnp.float32) * spread * level
    return jnp.minimum(jnp.maximum(array, -limit), limit).astype(kind)


def setup_inputs(seed: int = 0) -> dict:
    streams_of = jax.random.split(jax.random.key(seed), 9)
    candidate_rows = gaussian(streams_of[0], (CAND, D), 1.0, 6.0, ((0, 32),))
    weight_in = gaussian(streams_of[1], (LAYERS, D, HEADS, 4 * DH), D ** -0.5, 0.1875, ((2, 2),))
    weight_out = gaussian(streams_of[2], (LAYERS, HEADS, DH, D), (HEADS * DH) ** -0.5, 0.1875, ((1, 2),))
    history_cache = gaussian(streams_of[3], (LAYERS, 2, NROWS, HEADS, DH), 1.0, 6.0, ((2, 16), (3, 2)))
    block_user = draw_block_user(jax.random.fold_in(streams_of[8], 71), 0)
    block_offset = draw_block_offset(jax.random.fold_in(streams_of[8], 71), 0)
    history_length = draw_history_length(jax.random.fold_in(streams_of[8], 71), 0)
    candidate_count = draw_candidate_count(jax.random.fold_in(streams_of[8], 71), 0)
    return {"candidate_rows": candidate_rows, "weight_in": weight_in, "weight_out": weight_out, "history_cache": history_cache, "block_user": block_user, "block_offset": block_offset, "history_length": history_length, "candidate_count": candidate_count}


def reference(candidate_rows, weight_in, weight_out, history_cache, block_user, block_offset, history_length, candidate_count):
    score_scale = 1.0 / math.sqrt(DH)
    user_ends = jnp.cumsum(candidate_count)
    cand_user = lax.optimization_barrier(jnp.sum((jnp.arange(CAND, dtype=jnp.int32)[:, None] >= user_ends[None, :]).astype(jnp.int32), axis=1))
    users_all = jnp.arange(NU, dtype=jnp.int32)
    row_place = block_offset[:, None] * BLOCK + jnp.arange(BLOCK, dtype=jnp.int32)[None, :]
    owner_length = lax.optimization_barrier(jnp.sum(jnp.where(block_user[:, None] == users_all[None, :], history_length[None, :], 0), axis=1))
    row_valid = row_place < owner_length[:, None]
    cand_block = 512 if CAND % 512 == 0 else CAND
    group_width = HEADS // N_CAND * DH
    current = candidate_rows
    for layer_index in range(LAYERS):
        flat = weight_in[layer_index].reshape(D, HEADS * 4 * DH)
        mixed = jnp.dot(current, flat, preferred_element_type=jnp.float32)
        projected = jax.nn.silu(mixed).astype(jnp.bfloat16).reshape(CAND, HEADS, 4, DH)
        gate_part = projected[:, :, 0]
        values_part = projected[:, :, 1]
        queries = projected[:, :, 2]
        keys_part = projected[:, :, 3]
        key_blocks = history_cache[layer_index, 0].reshape(NBLK, BLOCK, HEADS, DH)
        value_blocks = history_cache[layer_index, 1].reshape(NBLK, BLOCK, HEADS, DH)

        def attend_group(inputs):
            query_group, user_group = inputs

            def visit_block(running, block_inputs):
                key_block, value_block, block_owner, valid_rows = block_inputs
                visible = (user_group[:, None] == block_owner) & valid_rows[None, :]

                def compute(running_sum):
                    scores = jnp.einsum('rhd,nhd->hrn', query_group.astype(jnp.float32), key_block.astype(jnp.float32)) * score_scale
                    weights = jnp.where(visible[None], jax.nn.silu(scores), 0.0).astype(jnp.bfloat16)
                    return running_sum + jnp.einsum('hrn,nhd->rhd', weights.astype(jnp.float32), value_block.astype(jnp.float32))

                def unchanged(running_sum):
                    return running_sum
                return (lax.cond(jnp.any(visible), compute, unchanged, running), None)
            initial = jnp.zeros((cand_block, HEADS, DH), jnp.float32)
            result, unused = lax.scan(visit_block, initial, (key_blocks, value_blocks, block_user, row_valid))
            return result
        attended = lax.map(attend_group, (queries.reshape(CAND // cand_block, cand_block, HEADS, DH), cand_user.reshape(CAND // cand_block, cand_block)))
        attended = attended.reshape(CAND, HEADS, DH)
        own_score = lax.optimization_barrier(jnp.sum(queries.astype(jnp.float32) * keys_part.astype(jnp.float32), axis=-1)) * score_scale
        own_weight = jax.nn.silu(own_score).astype(jnp.bfloat16)
        attended = attended + own_weight.astype(jnp.float32)[..., None] * values_part.astype(jnp.float32)
        centred = attended - lax.optimization_barrier(jnp.mean(attended, axis=-1, keepdims=True))
        variance = lax.optimization_barrier(jnp.mean(centred * centred, axis=-1, keepdims=True))
        gated = (centred * lax.rsqrt(variance + 1e-05) * gate_part.astype(jnp.float32)).astype(jnp.bfloat16)
        gated_flat = gated.reshape(CAND, HEADS * DH)
        out_flat = weight_out[layer_index].reshape(HEADS * DH, D)
        total = current.astype(jnp.float32)
        for group_index in range(N_CAND):
            group_in = gated_flat[:, group_index * group_width:(group_index + 1) * group_width]
            group_weight = out_flat[group_index * group_width:(group_index + 1) * group_width]
            group_term = jnp.dot(group_in, group_weight, preferred_element_type=jnp.float32).astype(jnp.bfloat16)
            group_term = lax.optimization_barrier(group_term)
            total = total + group_term.astype(jnp.float32)
        current = total.astype(jnp.bfloat16)
    return current
```

```python
import functools
import math

import jax
import jax.numpy as jnp
from jax import lax
from jax.experimental import pallas as pl
from jax.experimental.pallas import tpu as pltpu
from jax.sharding import PartitionSpec as P

BLOCK = 128
LANES = 128
FAR = -1e30
MIB = 1024 * 1024

VMEM_SPEC = pl.BlockSpec(memory_space=pltpu.VMEM)
SMEM_SPEC = pl.BlockSpec(memory_space=pltpu.SMEM)


def half_silu(half):
    return half + half * jnp.tanh(half)


def position(spot_bits):
    chip = lax.axis_index("users")
    spot = sum((((chip >> b) & 1) << i for i, b in enumerate(spot_bits)), chip * 0)
    return chip, spot, lax.axis_index("cand")


def order_history_kernel(spot_bits, h_ref, *refs):
    o_refs, pieces = refs[:-1], refs[-1]
    _, spot, _ = position(spot_bits)
    for layer_index in range(h_ref.shape[0]):
        for kind in range(h_ref.shape[1]):
            for head in range(h_ref.shape[3]):
                pieces[spot ^ head, layer_index, kind] = h_ref[layer_index, kind, :, head, :]
    for step, o_ref in enumerate(o_refs):
        o_ref[...] = pieces[step]


def join_layers_kernel(count, *refs):
    every_ref, *layer_refs = refs[count:]
    for layer_index, o_ref in enumerate(layer_refs):
        for at, ref in enumerate(refs[:count]):
            every_ref[layer_index, at] = ref[layer_index]
            o_ref[at] = ref[layer_index]


def halves_kernel(i_ref, low_ref, high_ref):
    size = low_ref.shape[0]
    low_ref[...] = i_ref[:size]
    high_ref[...] = i_ref[size:]


def join_kernel(*refs):
    o_ref = refs[-1]
    for at, ref in enumerate(refs[:-1]):
        o_ref[at] = ref[...]


def pick_head_kernel(layer_index, spot_bits, w_ref, o_ref, held, sems):
    _, spot, _ = position(spot_bits)
    chunks, rows = held.shape[:2]
    copies = [
        pltpu.make_async_copy(
            w_ref.at[layer_index, pl.ds(at * rows, rows)], held.at[at], sems.at[at]
        )
        for at in range(chunks)
    ]
    for copy in copies:
        copy.start()
    for at, copy in enumerate(copies):
        copy.wait()
        for head in range(held.shape[2]):

            @pl.when(spot == head)
            def _(at=at, head=head):
                o_ref[at * rows : (at + 1) * rows] = held[at, :, head, :]


def project(x_ref, w_ref, q_ref, gate_ref, own_ref, score_scale):
    dim = q_ref.shape[1]

    def part(first):
        w = w_ref[:, first * dim : (first + 2) * dim]
        mixed = jnp.dot(x_ref[...], w, preferred_element_type=jnp.float32)
        return half_silu(mixed * 0.5).astype(jnp.bfloat16)

    tail = part(2)
    query = tail[:, :dim]
    q_ref[...] = query
    score = jnp.sum(
        query.astype(jnp.float32) * tail[:, dim:].astype(jnp.float32), axis=-1, keepdims=True
    )
    weight = half_silu(score * (0.5 * score_scale)).astype(jnp.bfloat16).astype(jnp.float32)
    front = part(0)
    gate_ref[...] = front[:, :dim]
    own_ref[...] = weight * front[:, dim:].astype(jnp.float32)


def begin_kernel(spots, cores, spot_bits, score_scale, *refs):
    _, spot, core_here = position(spot_bits)
    x_refs, (w_ref, x_out, q_ref, gate_ref, own_ref) = refs[:-5], refs[-5:]
    own_rows = x_out.shape[0] // (spots * cores)
    for shift in range(cores):
        core = lax.rem(core_here + (cores - shift), cores)
        for step in range(spots):
            if shift == 0:
                piece = x_refs[step][...]
            else:
                piece = x_refs[spots + shift - 1][step]
            at = ((spot ^ step) * cores + core) * own_rows
            x_out[pl.ds(pl.multiple_of(at, own_rows), own_rows)] = piece
    project(x_out, w_ref, q_ref, gate_ref, own_ref, score_scale)


def gather_heads(gated_refs, spot, wide):
    dim = gated_refs[0].shape[1]
    for step, ref in enumerate(gated_refs):
        at = pl.multiple_of((spot ^ step) * dim, dim)
        wide[:, pl.ds(at, dim)] = ref[...]


def term_kernel(spots, spot_bits, layer_index, *refs):
    _, spot, _ = position(spot_bits)
    gated_refs, (weight_ref, o_ref, wide) = refs[:spots], refs[spots:]
    gather_heads(gated_refs, spot, wide)
    depth, width = wide.shape[1], o_ref.shape[1]
    tile = min(width, 256)
    for first in range(0, width, tile):
        columns = slice(first, first + tile)
        weight = weight_ref[layer_index, :, :, columns].reshape(depth, tile)
        o_ref[:, columns] = jnp.dot(
            wide[...], weight, preferred_element_type=jnp.float32
        ).astype(jnp.bfloat16)


def step_kernel(spots, cores, spot_bits, score_scale, *refs):
    _, spot, core = position(spot_bits)
    term_refs, (x_ref, w_ref, x_own, q_ref, gate_ref, own_ref, x_next) = refs[:cores], refs[cores:]
    total = x_ref[...].astype(jnp.float32)
    for ref in term_refs:
        total = total + ref[...].astype(jnp.float32)
    x_next[...] = total.astype(jnp.bfloat16)
    own_rows = x_own.shape[0]
    at = (spot * cores + core) * own_rows
    x_own[...] = x_next[pl.ds(pl.multiple_of(at, own_rows), own_rows)]
    project(x_next, w_ref, q_ref, gate_ref, own_ref, score_scale)


def last_term_kernel(spots, cores, spot_bits, layer_index, *refs):
    _, spot, core = position(spot_bits)
    gated_refs, (weight_ref, *o_refs, wide, total) = refs[:spots], refs[spots:]
    gather_heads(gated_refs, spot, wide)
    own_rows, width = o_refs[0].shape
    weight = weight_ref[layer_index].reshape(wide.shape[1], width)
    total[...] = jnp.dot(wide[...], weight, preferred_element_type=jnp.float32)
    for shift, o_ref in enumerate(o_refs):
        at = lax.rem(core + shift, cores) * own_rows
        o_ref[...] = total[pl.ds(pl.multiple_of(at, own_rows), own_rows)].astype(jnp.bfloat16)


def add_kernel(*refs):
    total = refs[0][...].astype(jnp.float32)
    for ref in refs[1:-1]:
        total = total + ref[...].astype(jnp.float32)
    refs[-1][...] = total.astype(jnp.bfloat16)


def visit_history(spot_bits, masks, held, layer_index, scalar_refs, history_refs, q_wide, total):
    user_ref, offset_ref, length_ref = scalar_refs
    spot_masks, member_masks, spot_of_chip, row_count = masks
    spots = len(spot_masks)
    dim = total.shape[1]
    scale = 0.5 / math.sqrt(dim)
    chip, _, _ = position(spot_bits)
    spot_part = chip & spot_of_chip
    member_part = chip - spot_part
    history_refs = [ref if len(ref.shape) == 4 else ref.at[layer_index] for ref in history_refs]

    def visit(ref, first, count, member, at):
        keys, values = [], []
        for piece in range(count):
            for block in range(ref.shape[2] // BLOCK):
                source = (member | (spot_part ^ spot_masks[at + piece])) * (ref.shape[2] // BLOCK) + block
                owner = user_ref[source]
                limit = length_ref[owner] - offset_ref[source] * BLOCK
                lanes = lax.broadcasted_iota(jnp.int32, (BLOCK, LANES), 1)
                sublanes = lax.broadcasted_iota(jnp.int32, (BLOCK, LANES), 0)
                seen = (lanes == owner) & (sublanes < limit)
                side = jnp.where(seen, 0.0, FAR).astype(jnp.bfloat16)
                at_rows = pl.ds(block * BLOCK, BLOCK)
                keys.append(jnp.concatenate([ref[first + piece, 0, at_rows], side], axis=1))
                values.append(ref[first + piece, 1, at_rows])
        half = lax.dot_general(
            q_wide[...],
            jnp.concatenate(keys, axis=0),
            (((1,), (1,)), ((), ())),
            preferred_element_type=jnp.float32,
        )
        weights = half_silu(half * scale).astype(jnp.bfloat16)
        total[...] += jnp.dot(
            weights, jnp.concatenate(values, axis=0), preferred_element_type=jnp.float32
        )

    if len(history_refs) == len(held):
        for ref, (mask, at) in zip(history_refs, held):
            visit(ref, 0, ref.shape[0], member_part ^ mask, at)
    else:

        @pl.loop(0, len(member_masks))
        def _(turn):
            member = turn * 0
            for i in range((len(member_masks) - 1).bit_length()):
                member = member | (((turn >> i) & 1) * member_masks[1 << i])
            visit(history_refs[0], turn * spots, spots, member, 0)


def attend_kernel(spot_bits, masks, held, layer_index, *refs):
    user_ref, offset_ref, length_ref, count_ref, q_ref, own_ref = refs[:6]
    history_refs, (q_wide, total) = refs[6:-2], refs[-2:]
    spot_masks, member_masks, spot_of_chip, row_count = masks
    spots = len(spot_masks)
    rows = q_ref.shape[0] // spots
    dim = q_ref.shape[1]
    user_count = length_ref.shape[0]
    chip, _, _ = position(spot_bits)
    member_part = chip - (chip & spot_of_chip)
    lane = lax.broadcasted_iota(jnp.int32, (1, LANES), 1)
    starts = jnp.zeros((1, LANES), jnp.int32)
    ends = jnp.zeros((1, LANES), jnp.int32)
    running = jnp.int32(0)
    for user in range(user_count):
        starts = jnp.where(lane == user, running, starts)
        running = running + count_ref[user]
        ends = jnp.where(lane == user, running, ends)
    q_wide[:, :dim] = q_ref[...]
    for at in range(spots):
        first = (member_part | spot_masks[at]) * row_count
        index = first + lax.broadcasted_iota(jnp.int32, (rows, LANES), 0)
        mine = (index >= starts) & (index < ends)
        q_wide[at * rows : (at + 1) * rows, dim:] = jnp.where(mine, 1.0, 0.0).astype(
            jnp.bfloat16
        )
    total[...] = own_ref[...]
    visit_history(
        spot_bits,
        masks,
        held,
        layer_index,
        (user_ref, offset_ref, length_ref),
        history_refs,
        q_wide,
        total,
    )


def finish_kernel(spot_bits, masks, held, layer_index, last, *refs):
    scalar_refs, (q_wide, before_ref, gate_ref), refs = refs[:3], refs[3:6], refs[6:]
    spots = len(masks[0])
    outs = spots if last else 1
    history_refs, o_refs, total = refs[: -outs - 1], refs[-outs - 1 : -1], refs[-1]
    rows = before_ref.shape[0] // spots
    _, spot, _ = position(spot_bits)
    total[...] = before_ref[...]
    if history_refs:
        visit_history(
            spot_bits, masks, held, layer_index, scalar_refs, history_refs, q_wide, total
        )
    full = total[...]
    centred = full - jnp.mean(full, axis=-1, keepdims=True)
    variance = jnp.mean(centred * centred, axis=-1, keepdims=True)
    gated = centred * lax.rsqrt(variance + 1e-05) * gate_ref[...].astype(jnp.float32)
    if not last:
        o_refs[0][...] = gated.astype(jnp.bfloat16)
        return
    total[...] = gated
    for step in range(spots):
        at_rows = pl.ds(pl.multiple_of((spot ^ step) * rows, rows), rows)
        o_refs[step][...] = total[at_rows].astype(jnp.bfloat16)


def body(
    candidate_rows,
    weight_in,
    weight_out,
    history_cache,
    block_user,
    block_offset,
    history_length,
    candidate_count,
):
    own_rows, model_width = candidate_rows.shape
    layers, model_again, heads_here, packed = weight_in.shape
    head_dim = packed // 4
    local_rows = history_cache.shape[2]
    cores = lax.axis_size("cand")
    chips = lax.axis_size("users")
    spots = heads_here
    groups = chips // spots
    row_count = own_rows * cores
    all_rows = row_count * spots
    score_scale = 1.0 / math.sqrt(head_dim)

    bits = list(range(chips.bit_length() - 1))
    spot_bits = sorted((bits[::2] + bits[1::2])[: spots.bit_length() - 1])
    member_bits = [b for b in bits if b not in spot_bits]

    def mask_of(number, places):
        return sum(((number >> i) & 1) << b for i, b in enumerate(places))

    def swap(value, mask):
        return lax.ppermute(value, "users", [(u, u ^ mask) for u in range(chips)])

    def trade_spots(values):
        return [values[0]] + [swap(values[m], mask_of(m, spot_bits)) for m in range(1, spots)]

    def gather_spots(value):
        found = [value]
        for bit in reversed(range(len(spot_bits))):
            mask = 1 << spot_bits[bit]
            found = [(v, swap(v, mask)) for v in found]
            found = [v for v, _ in found] + [w for _, w in found]
        order = [0]
        for bit in reversed(range(len(spot_bits))):
            order = order + [o | (1 << bit) for o in order]
        return [found[order.index(m)] for m in range(spots)]

    def shift_core(value, step):
        pairs = [(c, (c + step) % cores) for c in range(cores)]
        return lax.ppermute(value, "cand", pairs)

    spot_masks = [mask_of(m, spot_bits) for m in range(spots)]
    member_masks = [mask_of(m, member_bits) for m in range(groups)]

    masks = (spot_masks, member_masks, spot_masks[-1], row_count)

    def gather_members(pieces):
        if groups <= 2:
            return [pieces] + [swap(pieces, mask) for mask in member_masks[1:]]
        chips_of = [[mask_of(s, spot_bits) | m for m in member_masks] for s in range(spots)]
        return [
            lax.all_gather(pieces, "users", axis=0, axis_index_groups=chips_of, tiled=True)
        ]

    def after(value, *others):
        return lax.optimization_barrier((value,) + others)[0]

    def kernel_call(kernel, outs, name, operands, scratch=(), limit=8, specs=None):
        results = pl.pallas_call(
            kernel,
            out_shape=[jax.ShapeDtypeStruct(*out) for out in outs],
            in_specs=specs or [VMEM_SPEC] * len(operands),
            out_specs=[VMEM_SPEC] * len(outs),
            scratch_shapes=scratch,
            compiler_params=pltpu.CompilerParams(vmem_limit_bytes=limit * MIB),
            name=name,
        )(*operands)
        return list(results)

    def pick_head(layer_index):
        rows = min(model_width, 128)
        chunks = model_width // rows
        return kernel_call(
            functools.partial(pick_head_kernel, layer_index, spot_bits),
            [((model_width, packed), weight_in.dtype)],
            "pick_head",
            [weight_in],
            [
                pltpu.VMEM((chunks, rows, heads_here, packed), weight_in.dtype),
                pltpu.SemaphoreType.DMA((chunks,)),
            ],
            51,
            [pl.BlockSpec(memory_space=pl.ANY)],
        )[0]

    def order_history():
        shape = (layers, 2, local_rows, head_dim)
        return kernel_call(
            functools.partial(order_history_kernel, spot_bits),
            [(shape, jnp.bfloat16)] * spots,
            "order_history",
            [history_cache],
            [pltpu.VMEM((spots,) + shape, jnp.bfloat16)],
            4,
        )

    def join_layers(pieces):
        shape = (spots, 2, local_rows, head_dim)
        every, first, *later = kernel_call(
            functools.partial(join_layers_kernel, spots),
            [((layers,) + shape, jnp.bfloat16)] + [(shape, jnp.bfloat16)] * layers,
            "join_layers",
            list(pieces),
        )
        return every, first, later

    def halves(pieces):
        shape = (pieces.shape[0] // 2,) + pieces.shape[1:]
        return kernel_call(halves_kernel, [(shape, pieces.dtype)] * 2, "halves", [pieces])

    def join(pieces):
        if len(pieces) == 1:
            return pieces[0][None]
        shape = (len(pieces),) + pieces[0].shape
        return kernel_call(join_kernel, [(shape, pieces[0].dtype)], "join", list(pieces))[0]

    def together(*values):
        return lax.optimization_barrier(values)

    pieces, first_weight = together(trade_spots(order_history()), pick_head(0))
    every, first, later = join_layers(pieces)
    x_pieces = trade_spots([after(candidate_rows, first)] * spots)
    crossed = groups == 4
    if crossed:
        near_mask, far_mask = member_masks[1:3]
        far, near, x_pieces = together(
            swap(first, far_mask), swap(every, near_mask), x_pieces
        )
        history = [[every, near, far, swap(far, near_mask)]]
    else:
        history = [gather_members(first)]
    x_group = x_pieces + [shift_core(join(x_pieces), s) for s in range(1, cores)]

    scalars = [block_user, block_offset, history_length, candidate_count]
    one_head = (all_rows, head_dim)
    head_outs = [(one_head, jnp.bfloat16), (one_head, jnp.bfloat16), (one_head, jnp.float32)]
    x, *projected = kernel_call(
        functools.partial(begin_kernel, spots, cores, spot_bits, score_scale),
        [((all_rows, model_width), jnp.bfloat16)] + head_outs,
        "begin",
        x_group + [first_weight],
    )

    for layer_index in range(layers):
        last = layer_index + 1 == layers
        outs = [((row_count, head_dim), jnp.bfloat16)] * spots if last else head_outs[:1]
        query, gate, own = projected
        held, split = (), 1
        if crossed:
            parts = 2 if layer_index else 1
            cuts = [spots // parts * part for part in range(parts)]
            held = ((0, 0), (near_mask, 0))
            held += tuple((m, at) for m in (far_mask, near_mask | far_mask) for at in cuts)
            split = 2 + parts + parts // 2
        ready, coming = history[layer_index][:split], history[layer_index][split:]
        operands = scalars + [query, own] + ready
        wide_query, total = kernel_call(
            functools.partial(attend_kernel, spot_bits, masks, held[:split], layer_index),
            [((all_rows, head_dim + LANES), jnp.bfloat16), (one_head, jnp.float32)],
            "attend",
            operands,
            (),
            16,
            [SMEM_SPEC] * 4 + [VMEM_SPEC] * (len(operands) - 4),
        )
        operands = scalars[:3] + [wide_query, total, gate] + coming
        gated = kernel_call(
            functools.partial(finish_kernel, spot_bits, masks, held[split:], layer_index, last),
            outs,
            "finish",
            operands,
            [pltpu.VMEM(one_head, jnp.float32)],
            16,
            [SMEM_SPEC] * 3 + [VMEM_SPEC] * (len(operands) - 3),
        )
        if not last:
            gated = trade_spots(list(gated) * spots)
            next_weight = pick_head(layer_index + 1)
            if crossed:
                far = swap(after(later[layer_index], far), far_mask)
                far = halves(after(far, gated[1]))
                ahead = swap(far[0], near_mask)
                gated, far, ahead, next_weight = together(gated, far, ahead, next_weight)
                arrays = [every, near] + far + [ahead, swap(far[1], near_mask)]
            else:
                arrays = gather_members(later[layer_index])
            terms = kernel_call(
                functools.partial(term_kernel, spots, spot_bits, layer_index),
                [((all_rows, model_width), jnp.bfloat16)],
                "term",
                gated + [weight_out],
                [pltpu.VMEM((all_rows, spots * head_dim), jnp.bfloat16)],
            )
            terms = terms + [shift_core(terms[0], s) for s in range(1, cores)]
            history.append(arrays)
            x, *projected = kernel_call(
                functools.partial(step_kernel, spots, cores, spot_bits, score_scale),
                [((own_rows, model_width), jnp.bfloat16)] + head_outs,
                "step",
                terms + [x, next_weight],
                [pltpu.VMEM((all_rows, model_width), jnp.bfloat16)],
                12,
            )
        else:
            terms = kernel_call(
                functools.partial(last_term_kernel, spots, cores, spot_bits, layer_index),
                [((own_rows, model_width), jnp.bfloat16)] * cores,
                "last_term",
                trade_spots(gated) + [weight_out],
                [
                    pltpu.VMEM((row_count, spots * head_dim), jnp.bfloat16),
                    pltpu.VMEM((row_count, model_width), jnp.float32),
                ],
            )
            terms = terms[:1] + [shift_core(terms[s], s) for s in range(1, cores)]
            (out,) = kernel_call(
                add_kernel, [((own_rows, model_width), jnp.bfloat16)], "add", [x] + terms
            )
    return out


def solution(mesh):
    placed = (
        P(("users", "cand"), None),
        P(None, None, "cand", None),
        P(None, "cand", None, None),
        P(None, None, "users", "cand", None),
        P(),
        P(),
        P(),
        P(),
    )
    return jax.shard_map(
        body, mesh=mesh, in_specs=placed, out_specs=P(("users", "cand"), None), check_vma=False
    )
```

```python
import functools
import math

import jax
import jax.numpy as jnp
from jax import lax
from jax.experimental import pallas as pl
from jax.experimental.pallas import tpu as pltpu
from jax.sharding import PartitionSpec as P

BLOCK = 128
LANES = 128
FAR = -1e30
MIB = 1024 * 1024

VMEM_SPEC = pl.BlockSpec(memory_space=pltpu.VMEM)
SMEM_SPEC = pl.BlockSpec(memory_space=pltpu.SMEM)


def half_silu(half):
    return half + half * jnp.tanh(half)


def position(spot_bits):
    chip = lax.axis_index("users")
    spot = sum((((chip >> b) & 1) << i for i, b in enumerate(spot_bits)), chip * 0)
    return chip, spot, lax.axis_index("cand")


def order_history_kernel(spot_bits, h_ref, *refs):
    o_refs, pieces = refs[:-1], refs[-1]
    _, spot, _ = position(spot_bits)
    for layer_index in range(h_ref.shape[0]):
        for kind in range(h_ref.shape[1]):
            for head in range(h_ref.shape[3]):
                pieces[spot ^ head, layer_index, kind] = h_ref[layer_index, kind, :, head, :]
    for step, o_ref in enumerate(o_refs):
        o_ref[...] = pieces[step]


def join_layers_kernel(count, *refs):
    for layer_index, o_ref in enumerate(refs[count:]):
        for at, ref in enumerate(refs[:count]):
            o_ref[at] = ref[layer_index]


def halves_kernel(i_ref, low_ref, high_ref):
    size = low_ref.shape[0]
    low_ref[...] = i_ref[:size]
    high_ref[...] = i_ref[size:]


def join_kernel(*refs):
    o_ref = refs[-1]
    for at, ref in enumerate(refs[:-1]):
        o_ref[at] = ref[...]


def pick_head_kernel(layer_index, spot_bits, w_ref, o_ref, held, sems):
    _, spot, _ = position(spot_bits)
    chunks, rows = held.shape[:2]
    copies = [
        pltpu.make_async_copy(
            w_ref.at[layer_index, pl.ds(at * rows, rows)], held.at[at], sems.at[at]
        )
        for at in range(chunks)
    ]
    for copy in copies:
        copy.start()
    for at, copy in enumerate(copies):
        copy.wait()
        for head in range(held.shape[2]):

            @pl.when(spot == head)
            def _(at=at, head=head):
                o_ref[at * rows : (at + 1) * rows] = held[at, :, head, :]


def project(x_ref, w_ref, q_ref, gate_ref, own_ref, score_scale):
    dim = q_ref.shape[1]

    def part(first):
        w = w_ref[:, first * dim : (first + 2) * dim]
        mixed = jnp.dot(x_ref[...], w, preferred_element_type=jnp.float32)
        return half_silu(mixed * 0.5).astype(jnp.bfloat16)

    tail = part(2)
    query = tail[:, :dim]
    q_ref[...] = query
    score = jnp.sum(
        query.astype(jnp.float32) * tail[:, dim:].astype(jnp.float32), axis=-1, keepdims=True
    )
    weight = half_silu(score * (0.5 * score_scale)).astype(jnp.bfloat16).astype(jnp.float32)
    front = part(0)
    gate_ref[...] = front[:, :dim]
    own_ref[...] = weight * front[:, dim:].astype(jnp.float32)


def begin_kernel(spots, cores, spot_bits, score_scale, *refs):
    _, spot, core_here = position(spot_bits)
    x_refs, (w_ref, x_out, q_ref, gate_ref, own_ref) = refs[:-5], refs[-5:]
    own_rows = x_out.shape[0] // (spots * cores)
    for shift in range(cores):
        core = lax.rem(core_here + (cores - shift), cores)
        for step in range(spots):
            if shift == 0:
                piece = x_refs[step][...]
            else:
                piece = x_refs[spots + shift - 1][step]
            at = ((spot ^ step) * cores + core) * own_rows
            x_out[pl.ds(pl.multiple_of(at, own_rows), own_rows)] = piece
    project(x_out, w_ref, q_ref, gate_ref, own_ref, score_scale)


def gather_heads(gated_refs, spot, wide):
    dim = gated_refs[0].shape[1]
    for step, ref in enumerate(gated_refs):
        at = pl.multiple_of((spot ^ step) * dim, dim)
        wide[:, pl.ds(at, dim)] = ref[...]


def term_kernel(spots, spot_bits, layer_index, *refs):
    _, spot, _ = position(spot_bits)
    gated_refs, (weight_ref, o_ref, wide) = refs[:spots], refs[spots:]
    gather_heads(gated_refs, spot, wide)
    depth, width = wide.shape[1], o_ref.shape[1]
    tile = min(width, 256)
    for first in range(0, width, tile):
        columns = slice(first, first + tile)
        weight = weight_ref[layer_index, :, :, columns].reshape(depth, tile)
        o_ref[:, columns] = jnp.dot(
            wide[...], weight, preferred_element_type=jnp.float32
        ).astype(jnp.bfloat16)


def step_kernel(spots, cores, spot_bits, score_scale, *refs):
    _, spot, core = position(spot_bits)
    term_refs, (x_ref, w_ref, x_own, q_ref, gate_ref, own_ref, x_next) = refs[:cores], refs[cores:]
    total = x_ref[...].astype(jnp.float32)
    for ref in term_refs:
        total = total + ref[...].astype(jnp.float32)
    x_next[...] = total.astype(jnp.bfloat16)
    own_rows = x_own.shape[0]
    at = (spot * cores + core) * own_rows
    x_own[...] = x_next[pl.ds(pl.multiple_of(at, own_rows), own_rows)]
    project(x_next, w_ref, q_ref, gate_ref, own_ref, score_scale)


def last_term_kernel(spots, cores, spot_bits, layer_index, *refs):
    _, spot, core = position(spot_bits)
    gated_refs, (weight_ref, *o_refs, wide, total) = refs[:spots], refs[spots:]
    gather_heads(gated_refs, spot, wide)
    own_rows, width = o_refs[0].shape
    weight = weight_ref[layer_index].reshape(wide.shape[1], width)
    total[...] = jnp.dot(wide[...], weight, preferred_element_type=jnp.float32)
    for shift, o_ref in enumerate(o_refs):
        at = lax.rem(core + shift, cores) * own_rows
        o_ref[...] = total[pl.ds(pl.multiple_of(at, own_rows), own_rows)].astype(jnp.bfloat16)


def add_kernel(*refs):
    total = refs[0][...].astype(jnp.float32)
    for ref in refs[1:-1]:
        total = total + ref[...].astype(jnp.float32)
    refs[-1][...] = total.astype(jnp.bfloat16)


def visit_history(spot_bits, masks, held, layer_index, scalar_refs, history_refs, q_wide, total):
    user_ref, offset_ref, length_ref = scalar_refs
    spot_masks, member_masks, spot_of_chip, row_count = masks
    spots = len(spot_masks)
    dim = total.shape[1]
    scale = 0.5 / math.sqrt(dim)
    chip, _, _ = position(spot_bits)
    spot_part = chip & spot_of_chip
    member_part = chip - spot_part

    def visit(ref, first, count, member, at):
        keys, values = [], []
        for piece in range(count):
            for block in range(ref.shape[2] // BLOCK):
                source = (member | (spot_part ^ spot_masks[at + piece])) * (ref.shape[2] // BLOCK) + block
                owner = user_ref[source]
                limit = length_ref[owner] - offset_ref[source] * BLOCK
                lanes = lax.broadcasted_iota(jnp.int32, (BLOCK, LANES), 1)
                sublanes = lax.broadcasted_iota(jnp.int32, (BLOCK, LANES), 0)
                seen = (lanes == owner) & (sublanes < limit)
                side = jnp.where(seen, 0.0, FAR).astype(jnp.bfloat16)
                at_rows = pl.ds(block * BLOCK, BLOCK)
                keys.append(jnp.concatenate([ref[first + piece, 0, at_rows], side], axis=1))
                values.append(ref[first + piece, 1, at_rows])
        half = lax.dot_general(
            q_wide[...],
            jnp.concatenate(keys, axis=0),
            (((1,), (1,)), ((), ())),
            preferred_element_type=jnp.float32,
        )
        weights = half_silu(half * scale).astype(jnp.bfloat16)
        total[...] += jnp.dot(
            weights, jnp.concatenate(values, axis=0), preferred_element_type=jnp.float32
        )

    if len(history_refs) == len(held):
        for ref, (mask, at) in zip(history_refs, held):
            visit(ref, 0, ref.shape[0], member_part ^ mask, at)
    else:

        @pl.loop(0, len(member_masks))
        def _(turn):
            member = turn * 0
            for i in range((len(member_masks) - 1).bit_length()):
                member = member | (((turn >> i) & 1) * member_masks[1 << i])
            visit(history_refs[0], turn * spots, spots, member, 0)


def attend_kernel(spot_bits, masks, held, layer_index, *refs):
    user_ref, offset_ref, length_ref, count_ref, q_ref, own_ref = refs[:6]
    history_refs, (q_wide, total) = refs[6:-2], refs[-2:]
    spot_masks, member_masks, spot_of_chip, row_count = masks
    spots = len(spot_masks)
    rows = q_ref.shape[0] // spots
    dim = q_ref.shape[1]
    user_count = length_ref.shape[0]
    chip, _, _ = position(spot_bits)
    member_part = chip - (chip & spot_of_chip)
    lane = lax.broadcasted_iota(jnp.int32, (1, LANES), 1)
    starts = jnp.zeros((1, LANES), jnp.int32)
    ends = jnp.zeros((1, LANES), jnp.int32)
    running = jnp.int32(0)
    for user in range(user_count):
        starts = jnp.where(lane == user, running, starts)
        running = running + count_ref[user]
        ends = jnp.where(lane == user, running, ends)
    q_wide[:, :dim] = q_ref[...]
    for at in range(spots):
        first = (member_part | spot_masks[at]) * row_count
        index = first + lax.broadcasted_iota(jnp.int32, (rows, LANES), 0)
        mine = (index >= starts) & (index < ends)
        q_wide[at * rows : (at + 1) * rows, dim:] = jnp.where(mine, 1.0, 0.0).astype(
            jnp.bfloat16
        )
    total[...] = own_ref[...]
    visit_history(
        spot_bits,
        masks,
        held,
        layer_index,
        (user_ref, offset_ref, length_ref),
        history_refs,
        q_wide,
        total,
    )


def finish_kernel(spot_bits, masks, held, layer_index, last, *refs):
    scalar_refs, (q_wide, before_ref, gate_ref), refs = refs[:3], refs[3:6], refs[6:]
    spots = len(masks[0])
    outs = spots if last else 1
    history_refs, o_refs, total = refs[: -outs - 1], refs[-outs - 1 : -1], refs[-1]
    rows = before_ref.shape[0] // spots
    _, spot, _ = position(spot_bits)
    total[...] = before_ref[...]
    if history_refs:
        visit_history(
            spot_bits, masks, held, layer_index, scalar_refs, history_refs, q_wide, total
        )
    full = total[...]
    centred = full - jnp.mean(full, axis=-1, keepdims=True)
    variance = jnp.mean(centred * centred, axis=-1, keepdims=True)
    gated = centred * lax.rsqrt(variance + 1e-05) * gate_ref[...].astype(jnp.float32)
    if not last:
        o_refs[0][...] = gated.astype(jnp.bfloat16)
        return
    total[...] = gated
    for step in range(spots):
        at_rows = pl.ds(pl.multiple_of((spot ^ step) * rows, rows), rows)
        o_refs[step][...] = total[at_rows].astype(jnp.bfloat16)


def body(
    candidate_rows,
    weight_in,
    weight_out,
    history_cache,
    block_user,
    block_offset,
    history_length,
    candidate_count,
):
    own_rows, model_width = candidate_rows.shape
    layers, model_again, heads_here, packed = weight_in.shape
    head_dim = packed // 4
    local_rows = history_cache.shape[2]
    cores = lax.axis_size("cand")
    chips = lax.axis_size("users")
    spots = heads_here
    groups = chips // spots
    row_count = own_rows * cores
    all_rows = row_count * spots
    score_scale = 1.0 / math.sqrt(head_dim)

    bits = list(range(chips.bit_length() - 1))
    spot_bits = sorted((bits[::2] + bits[1::2])[: spots.bit_length() - 1])
    member_bits = [b for b in bits if b not in spot_bits]

    def mask_of(number, places):
        return sum(((number >> i) & 1) << b for i, b in enumerate(places))

    def swap(value, mask):
        return lax.ppermute(value, "users", [(u, u ^ mask) for u in range(chips)])

    def trade_spots(values):
        return [values[0]] + [swap(values[m], mask_of(m, spot_bits)) for m in range(1, spots)]

    def gather_spots(value):
        found = [value]
        for bit in reversed(range(len(spot_bits))):
            mask = 1 << spot_bits[bit]
            found = [(v, swap(v, mask)) for v in found]
            found = [v for v, _ in found] + [w for _, w in found]
        order = [0]
        for bit in reversed(range(len(spot_bits))):
            order = order + [o | (1 << bit) for o in order]
        return [found[order.index(m)] for m in range(spots)]

    def shift_core(value, step):
        pairs = [(c, (c + step) % cores) for c in range(cores)]
        return lax.ppermute(value, "cand", pairs)

    spot_masks = [mask_of(m, spot_bits) for m in range(spots)]
    member_masks = [mask_of(m, member_bits) for m in range(groups)]

    masks = (spot_masks, member_masks, spot_masks[-1], row_count)

    def gather_members(pieces):
        if groups <= 2:
            return [pieces] + [swap(pieces, mask) for mask in member_masks[1:]]
        chips_of = [[mask_of(s, spot_bits) | m for m in member_masks] for s in range(spots)]
        return [
            lax.all_gather(pieces, "users", axis=0, axis_index_groups=chips_of, tiled=True)
        ]

    def after(value, *others):
        return lax.optimization_barrier((value,) + others)[0]

    def kernel_call(kernel, outs, name, operands, scratch=(), limit=8, specs=None):
        results = pl.pallas_call(
            kernel,
            out_shape=[jax.ShapeDtypeStruct(*out) for out in outs],
            in_specs=specs or [VMEM_SPEC] * len(operands),
            out_specs=[VMEM_SPEC] * len(outs),
            scratch_shapes=scratch,
            compiler_params=pltpu.CompilerParams(vmem_limit_bytes=limit * MIB),
            name=name,
        )(*operands)
        return list(results)

    def pick_head(layer_index):
        rows = min(model_width, 128)
        chunks = model_width // rows
        return kernel_call(
            functools.partial(pick_head_kernel, layer_index, spot_bits),
            [((model_width, packed), weight_in.dtype)],
            "pick_head",
            [weight_in],
            [
                pltpu.VMEM((chunks, rows, heads_here, packed), weight_in.dtype),
                pltpu.SemaphoreType.DMA((chunks,)),
            ],
            51,
            [pl.BlockSpec(memory_space=pl.ANY)],
        )[0]

    def order_history():
        shape = (layers, 2, local_rows, head_dim)
        return kernel_call(
            functools.partial(order_history_kernel, spot_bits),
            [(shape, jnp.bfloat16)] * spots,
            "order_history",
            [history_cache],
            [pltpu.VMEM((spots,) + shape, jnp.bfloat16)],
            4,
        )

    def join_layers(pieces):
        shape = (spots, 2, local_rows, head_dim)
        first, *later = kernel_call(
            functools.partial(join_layers_kernel, spots),
            [(shape, jnp.bfloat16)] * layers,
            "join_layers",
            list(pieces),
        )
        return first, later

    def halves(pieces):
        shape = (pieces.shape[0] // 2,) + pieces.shape[1:]
        return kernel_call(halves_kernel, [(shape, pieces.dtype)] * 2, "halves", [pieces])

    def join(pieces):
        if len(pieces) == 1:
            return pieces[0][None]
        shape = (len(pieces),) + pieces[0].shape
        return kernel_call(join_kernel, [(shape, pieces[0].dtype)], "join", list(pieces))[0]

    def together(*values):
        return lax.optimization_barrier(values)

    pieces, first_weight = together(trade_spots(order_history()), pick_head(0))
    first, later = join_layers(pieces)
    x_pieces = trade_spots([after(candidate_rows, first)] * spots)
    crossed = groups == 4
    if crossed:
        near_mask, far_mask = member_masks[1:3]
        far = swap(first, far_mask)
        near = swap(first, near_mask)
        far, near, x_pieces = together(far, near, x_pieces)
        history = [[first, near, far, swap(far, near_mask)]]
    else:
        history = [gather_members(first)]
    x_group = x_pieces + [shift_core(join(x_pieces), s) for s in range(1, cores)]

    scalars = [block_user, block_offset, history_length, candidate_count]
    one_head = (all_rows, head_dim)
    head_outs = [(one_head, jnp.bfloat16), (one_head, jnp.bfloat16), (one_head, jnp.float32)]
    x, *projected = kernel_call(
        functools.partial(begin_kernel, spots, cores, spot_bits, score_scale),
        [((all_rows, model_width), jnp.bfloat16)] + head_outs,
        "begin",
        x_group + [first_weight],
    )

    for layer_index in range(layers):
        last = layer_index + 1 == layers
        outs = [((row_count, head_dim), jnp.bfloat16)] * spots if last else head_outs[:1]
        query, gate, own = projected
        held, split = (), 1
        if crossed:
            parts = 2 if layer_index else 1
            cuts = [spots // parts * part for part in range(parts)]
            held = ((0, 0), (near_mask, 0))
            held += tuple((m, at) for m in (far_mask, near_mask | far_mask) for at in cuts)
            split = 2 + parts + parts // 2
        ready, coming = history[layer_index][:split], history[layer_index][split:]
        operands = scalars + [query, own] + ready
        wide_query, total = kernel_call(
            functools.partial(attend_kernel, spot_bits, masks, held[:split], layer_index),
            [((all_rows, head_dim + LANES), jnp.bfloat16), (one_head, jnp.float32)],
            "attend",
            operands,
            (),
            16,
            [SMEM_SPEC] * 4 + [VMEM_SPEC] * (len(operands) - 4),
        )
        operands = scalars[:3] + [wide_query, total, gate] + coming
        gated = kernel_call(
            functools.partial(finish_kernel, spot_bits, masks, held[split:], layer_index, last),
            outs,
            "finish",
            operands,
            [pltpu.VMEM(one_head, jnp.float32)],
            16,
            [SMEM_SPEC] * 3 + [VMEM_SPEC] * (len(operands) - 3),
        )
        if not last:
            gated = trade_spots(list(gated) * spots)
            next_weight = pick_head(layer_index + 1)
            if crossed:
                whole = after(later[layer_index], far, near)
                far, near = swap(whole, far_mask), swap(whole, near_mask)
                far = halves(after(far, near, gated[1]))
                ahead = swap(far[0], near_mask)
                gated, far, ahead, next_weight = together(gated, far, ahead, next_weight)
                arrays = [whole, near] + far + [ahead, swap(far[1], near_mask)]
            else:
                arrays = gather_members(later[layer_index])
            terms = kernel_call(
                functools.partial(term_kernel, spots, spot_bits, layer_index),
                [((all_rows, model_width), jnp.bfloat16)],
                "term",
                gated + [weight_out],
                [pltpu.VMEM((all_rows, spots * head_dim), jnp.bfloat16)],
            )
            terms = terms + [shift_core(terms[0], s) for s in range(1, cores)]
            history.append(arrays)
            x, *projected = kernel_call(
                functools.partial(step_kernel, spots, cores, spot_bits, score_scale),
                [((own_rows, model_width), jnp.bfloat16)] + head_outs,
                "step",
                terms + [x, next_weight],
                [pltpu.VMEM((all_rows, model_width), jnp.bfloat16)],
                12,
            )
        else:
            terms = kernel_call(
                functools.partial(last_term_kernel, spots, cores, spot_bits, layer_index),
                [((own_rows, model_width), jnp.bfloat16)] * cores,
                "last_term",
                trade_spots(gated) + [weight_out],
                [
                    pltpu.VMEM((row_count, spots * head_dim), jnp.bfloat16),
                    pltpu.VMEM((row_count, model_width), jnp.float32),
                ],
            )
            terms = terms[:1] + [shift_core(terms[s], s) for s in range(1, cores)]
            (out,) = kernel_call(
                add_kernel, [((own_rows, model_width), jnp.bfloat16)], "add", [x] + terms
            )
    return out


def solution(mesh):
    placed = (
        P(("users", "cand"), None),
        P(None, None, "cand", None),
        P(None, "cand", None, None),
        P(None, None, "users", "cand", None),
        P(),
        P(),
        P(),
        P(),
    )
    return jax.shard_map(
        body, mesh=mesh, in_specs=placed, out_specs=P(("users", "cand"), None), check_vma=False
    )
```

```python
import functools
import math

import jax
import jax.numpy as jnp
from jax import lax
from jax.experimental import pallas as pl
from jax.experimental.pallas import tpu as pltpu
from jax.sharding import PartitionSpec as P

BLOCK = 128
LANES = 128
FAR = -1e30
MIB = 1024 * 1024

VMEM_SPEC = pl.BlockSpec(memory_space=pltpu.VMEM)
SMEM_SPEC = pl.BlockSpec(memory_space=pltpu.SMEM)


def half_silu(half):
    return half + half * jnp.tanh(half)


def position(spot_bits):
    chip = lax.axis_index("users")
    spot = sum((((chip >> b) & 1) << i for i, b in enumerate(spot_bits)), chip * 0)
    return chip, spot, lax.axis_index("cand")


def order_history_kernel(spot_bits, h_ref, *refs):
    o_refs, pieces = refs[:-1], refs[-1]
    _, spot, _ = position(spot_bits)
    for layer_index in range(h_ref.shape[0]):
        for kind in range(h_ref.shape[1]):
            by_head = jnp.swapaxes(h_ref[layer_index, kind], 0, 1)
            for head in range(h_ref.shape[3]):
                pieces[spot ^ head, layer_index, kind] = by_head[head]
    for step, o_ref in enumerate(o_refs):
        o_ref[...] = pieces[step]


def join_layers_kernel(count, *refs):
    for layer_index, o_ref in enumerate(refs[count:]):
        for at, ref in enumerate(refs[:count]):
            o_ref[at] = ref[layer_index]


def halves_kernel(i_ref, low_ref, high_ref):
    size = low_ref.shape[0]
    low_ref[...] = i_ref[:size]
    high_ref[...] = i_ref[size:]


def join_kernel(*refs):
    o_ref = refs[-1]
    for at, ref in enumerate(refs[:-1]):
        o_ref[at] = ref[...]


def pick_head_kernel(layer_index, spot_bits, w_ref, o_ref, held, sems):
    _, spot, _ = position(spot_bits)
    chunks, rows = held.shape[:2]
    copies = [
        pltpu.make_async_copy(
            w_ref.at[layer_index, pl.ds(at * rows, rows)], held.at[at], sems.at[at]
        )
        for at in range(chunks)
    ]
    for copy in copies:
        copy.start()
    for at, copy in enumerate(copies):
        copy.wait()
        for head in range(held.shape[2]):

            @pl.when(spot == head)
            def _(at=at, head=head):
                o_ref[at * rows : (at + 1) * rows] = held[at, :, head, :]


def project(x_ref, w_ref, q_ref, gate_ref, own_ref, score_scale):
    dim = q_ref.shape[1]

    def part(first):
        w = w_ref[:, first * dim : (first + 2) * dim]
        mixed = jnp.dot(x_ref[...], w, preferred_element_type=jnp.float32)
        return half_silu(mixed * 0.5).astype(jnp.bfloat16)

    tail = part(2)
    query = tail[:, :dim]
    q_ref[...] = query
    score = jnp.sum(
        query.astype(jnp.float32) * tail[:, dim:].astype(jnp.float32), axis=-1, keepdims=True
    )
    weight = half_silu(score * (0.5 * score_scale)).astype(jnp.bfloat16).astype(jnp.float32)
    front = part(0)
    gate_ref[...] = front[:, :dim]
    own_ref[...] = weight * front[:, dim:].astype(jnp.float32)


def begin_kernel(spots, cores, spot_bits, score_scale, *refs):
    _, spot, core_here = position(spot_bits)
    x_refs, (w_ref, x_out, q_ref, gate_ref, own_ref) = refs[:-5], refs[-5:]
    own_rows = x_out.shape[0] // (spots * cores)
    for shift in range(cores):
        core = lax.rem(core_here + (cores - shift), cores)
        for step in range(spots):
            if shift == 0:
                piece = x_refs[step][...]
            else:
                piece = x_refs[spots + shift - 1][step]
            at = ((spot ^ step) * cores + core) * own_rows
            x_out[pl.ds(pl.multiple_of(at, own_rows), own_rows)] = piece
    project(x_out, w_ref, q_ref, gate_ref, own_ref, score_scale)


def gather_heads(gated_refs, spot, wide):
    dim = gated_refs[0].shape[1]
    for step, ref in enumerate(gated_refs):
        at = pl.multiple_of((spot ^ step) * dim, dim)
        wide[:, pl.ds(at, dim)] = ref[...]


def term_kernel(spot_bits, layer_index, first_step, *refs):
    _, spot, _ = position(spot_bits)
    count = len(refs) - 2 - (1 if first_step else 0)
    gated_refs, (weight_ref, *before_refs, o_ref) = refs[:count], refs[count:]
    gated = jnp.concatenate([ref[...] for ref in gated_refs], axis=1)
    width = o_ref.shape[1]
    tile = min(width, 256)
    for first in range(0, width, tile):
        columns = slice(first, first + tile)
        weight = jnp.concatenate(
            [weight_ref[layer_index, spot ^ (first_step + at), :, columns] for at in range(count)],
            axis=0,
        )
        term = jnp.dot(gated, weight, preferred_element_type=jnp.float32)
        if before_refs:
            term = term + before_refs[0][:, columns]
        o_ref[:, columns] = term.astype(o_ref.dtype)


def step_kernel(spots, cores, spot_bits, score_scale, *refs):
    _, spot, core = position(spot_bits)
    term_refs, (x_ref, w_ref, x_own, q_ref, gate_ref, own_ref, x_next) = refs[:cores], refs[cores:]
    total = x_ref[...].astype(jnp.float32)
    for ref in term_refs:
        total = total + ref[...].astype(jnp.float32)
    x_next[...] = total.astype(jnp.bfloat16)
    own_rows = x_own.shape[0]
    at = (spot * cores + core) * own_rows
    x_own[...] = x_next[pl.ds(pl.multiple_of(at, own_rows), own_rows)]
    project(x_next, w_ref, q_ref, gate_ref, own_ref, score_scale)


def last_term_kernel(spots, cores, spot_bits, layer_index, *refs):
    _, spot, core = position(spot_bits)
    gated_refs, (weight_ref, *o_refs, wide, total) = refs[:spots], refs[spots:]
    gather_heads(gated_refs, spot, wide)
    own_rows, width = o_refs[0].shape
    weight = weight_ref[layer_index].reshape(wide.shape[1], width)
    total[...] = jnp.dot(wide[...], weight, preferred_element_type=jnp.float32)
    for shift, o_ref in enumerate(o_refs):
        at = lax.rem(core + shift, cores) * own_rows
        o_ref[...] = total[pl.ds(pl.multiple_of(at, own_rows), own_rows)].astype(jnp.bfloat16)


def add_kernel(*refs):
    total = refs[0][...].astype(jnp.float32)
    for ref in refs[1:-1]:
        total = total + ref[...].astype(jnp.float32)
    refs[-1][...] = total.astype(jnp.bfloat16)


def visit_history(spot_bits, masks, held, layer_index, scalar_refs, history_refs, q_wide, total):
    user_ref, offset_ref, length_ref = scalar_refs
    spot_masks, member_masks, spot_of_chip, row_count = masks
    spots = len(spot_masks)
    dim = total.shape[1]
    scale = 0.5 / math.sqrt(dim)
    chip, _, _ = position(spot_bits)
    spot_part = chip & spot_of_chip
    member_part = chip - spot_part

    def visit(ref, first, count, member, at):
        keys, values = [], []
        for piece in range(count):
            for block in range(ref.shape[2] // BLOCK):
                source = (member | (spot_part ^ spot_masks[at + piece])) * (ref.shape[2] // BLOCK) + block
                owner = user_ref[source]
                limit = length_ref[owner] - offset_ref[source] * BLOCK
                lanes = lax.broadcasted_iota(jnp.int32, (BLOCK, LANES), 1)
                sublanes = lax.broadcasted_iota(jnp.int32, (BLOCK, LANES), 0)
                seen = (lanes == owner) & (sublanes < limit)
                side = jnp.where(seen, 0.0, FAR).astype(jnp.bfloat16)
                at_rows = pl.ds(block * BLOCK, BLOCK)
                keys.append(jnp.concatenate([ref[first + piece, 0, at_rows], side], axis=1))
                values.append(ref[first + piece, 1, at_rows])
        half = lax.dot_general(
            q_wide[...],
            jnp.concatenate(keys, axis=0),
            (((1,), (1,)), ((), ())),
            preferred_element_type=jnp.float32,
        )
        weights = half_silu(half * scale).astype(jnp.bfloat16)
        total[...] += jnp.dot(
            weights, jnp.concatenate(values, axis=0), preferred_element_type=jnp.float32
        )

    if len(history_refs) == len(held):
        for ref, (mask, at) in zip(history_refs, held):
            visit(ref, 0, ref.shape[0], member_part ^ mask, at)
    else:

        @pl.loop(0, len(member_masks))
        def _(turn):
            member = turn * 0
            for i in range((len(member_masks) - 1).bit_length()):
                member = member | (((turn >> i) & 1) * member_masks[1 << i])
            visit(history_refs[0], turn * spots, spots, member, 0)


def attend_kernel(spot_bits, masks, held, layer_index, *refs):
    user_ref, offset_ref, length_ref, count_ref, q_ref, own_ref = refs[:6]
    history_refs, (q_wide, total) = refs[6:-2], refs[-2:]
    spot_masks, member_masks, spot_of_chip, row_count = masks
    spots = len(spot_masks)
    rows = q_ref.shape[0] // spots
    dim = q_ref.shape[1]
    user_count = length_ref.shape[0]
    chip, _, _ = position(spot_bits)
    member_part = chip - (chip & spot_of_chip)
    lane = lax.broadcasted_iota(jnp.int32, (1, LANES), 1)
    starts = jnp.zeros((1, LANES), jnp.int32)
    ends = jnp.zeros((1, LANES), jnp.int32)
    running = jnp.int32(0)
    for user in range(user_count):
        starts = jnp.where(lane == user, running, starts)
        running = running + count_ref[user]
        ends = jnp.where(lane == user, running, ends)
    q_wide[:, :dim] = q_ref[...]
    for at in range(spots):
        first = (member_part | spot_masks[at]) * row_count
        index = first + lax.broadcasted_iota(jnp.int32, (rows, LANES), 0)
        mine = (index >= starts) & (index < ends)
        q_wide[at * rows : (at + 1) * rows, dim:] = jnp.where(mine, 1.0, 0.0).astype(
            jnp.bfloat16
        )
    total[...] = own_ref[...]
    visit_history(
        spot_bits,
        masks,
        held,
        layer_index,
        (user_ref, offset_ref, length_ref),
        history_refs,
        q_wide,
        total,
    )


def finish_kernel(spot_bits, masks, held, layer_index, last, *refs):
    scalar_refs, (q_wide, before_ref, gate_ref), refs = refs[:3], refs[3:6], refs[6:]
    spots = len(masks[0])
    outs = spots if last else 1
    history_refs, o_refs, total = refs[: -outs - 1], refs[-outs - 1 : -1], refs[-1]
    rows = before_ref.shape[0] // spots
    _, spot, _ = position(spot_bits)
    total[...] = before_ref[...]
    if history_refs:
        visit_history(
            spot_bits, masks, held, layer_index, scalar_refs, history_refs, q_wide, total
        )
    full = total[...]
    centred = full - jnp.mean(full, axis=-1, keepdims=True)
    variance = jnp.mean(centred * centred, axis=-1, keepdims=True)
    gated = centred * lax.rsqrt(variance + 1e-05) * gate_ref[...].astype(jnp.float32)
    if not last:
        o_refs[0][...] = gated.astype(jnp.bfloat16)
        return
    total[...] = gated
    for step in range(spots):
        at_rows = pl.ds(pl.multiple_of((spot ^ step) * rows, rows), rows)
        o_refs[step][...] = total[at_rows].astype(jnp.bfloat16)


def body(
    candidate_rows,
    weight_in,
    weight_out,
    history_cache,
    block_user,
    block_offset,
    history_length,
    candidate_count,
):
    own_rows, model_width = candidate_rows.shape
    layers, model_again, heads_here, packed = weight_in.shape
    head_dim = packed // 4
    local_rows = history_cache.shape[2]
    cores = lax.axis_size("cand")
    chips = lax.axis_size("users")
    spots = heads_here
    groups = chips // spots
    row_count = own_rows * cores
    all_rows = row_count * spots
    score_scale = 1.0 / math.sqrt(head_dim)

    bits = list(range(chips.bit_length() - 1))
    spot_bits = sorted((bits[::2] + bits[1::2])[: spots.bit_length() - 1])
    member_bits = [b for b in bits if b not in spot_bits]

    def mask_of(number, places):
        return sum(((number >> i) & 1) << b for i, b in enumerate(places))

    def swap(value, mask):
        return lax.ppermute(value, "users", [(u, u ^ mask) for u in range(chips)])

    def trade_spots(values):
        return [values[0]] + [swap(values[m], mask_of(m, spot_bits)) for m in range(1, spots)]

    def gather_spots(value):
        found = [value]
        for bit in reversed(range(len(spot_bits))):
            mask = 1 << spot_bits[bit]
            found = [(v, swap(v, mask)) for v in found]
            found = [v for v, _ in found] + [w for _, w in found]
        order = [0]
        for bit in reversed(range(len(spot_bits))):
            order = order + [o | (1 << bit) for o in order]
        return [found[order.index(m)] for m in range(spots)]

    def shift_core(value, step):
        pairs = [(c, (c + step) % cores) for c in range(cores)]
        return lax.ppermute(value, "cand", pairs)

    spot_masks = [mask_of(m, spot_bits) for m in range(spots)]
    member_masks = [mask_of(m, member_bits) for m in range(groups)]

    masks = (spot_masks, member_masks, spot_masks[-1], row_count)

    def gather_members(pieces):
        if groups <= 2:
            return [pieces] + [swap(pieces, mask) for mask in member_masks[1:]]
        chips_of = [[mask_of(s, spot_bits) | m for m in member_masks] for s in range(spots)]
        return [
            lax.all_gather(pieces, "users", axis=0, axis_index_groups=chips_of, tiled=True)
        ]

    def after(value, *others):
        return lax.optimization_barrier((value,) + others)[0]

    def kernel_call(kernel, outs, name, operands, scratch=(), limit=8, specs=None):
        results = pl.pallas_call(
            kernel,
            out_shape=[jax.ShapeDtypeStruct(*out) for out in outs],
            in_specs=specs or [VMEM_SPEC] * len(operands),
            out_specs=[VMEM_SPEC] * len(outs),
            scratch_shapes=scratch,
            compiler_params=pltpu.CompilerParams(vmem_limit_bytes=limit * MIB),
            name=name,
        )(*operands)
        return list(results)

    def pick_head(layer_index):
        rows = min(model_width, 128)
        chunks = model_width // rows
        return kernel_call(
            functools.partial(pick_head_kernel, layer_index, spot_bits),
            [((model_width, packed), weight_in.dtype)],
            "pick_head",
            [weight_in],
            [
                pltpu.VMEM((chunks, rows, heads_here, packed), weight_in.dtype),
                pltpu.SemaphoreType.DMA((chunks,)),
            ],
            51,
            [pl.BlockSpec(memory_space=pl.ANY)],
        )[0]

    def order_history():
        shape = (layers, 2, local_rows, head_dim)
        return kernel_call(
            functools.partial(order_history_kernel, spot_bits),
            [(shape, jnp.bfloat16)] * spots,
            "order_history",
            [history_cache],
            [pltpu.VMEM((spots,) + shape, jnp.bfloat16)],
            4,
        )

    def join_layers(pieces):
        shape = (spots, 2, local_rows, head_dim)
        first, *later = kernel_call(
            functools.partial(join_layers_kernel, spots),
            [(shape, jnp.bfloat16)] * layers,
            "join_layers",
            list(pieces),
        )
        return first, later

    def halves(pieces):
        shape = (pieces.shape[0] // 2,) + pieces.shape[1:]
        return kernel_call(halves_kernel, [(shape, pieces.dtype)] * 2, "halves", [pieces])

    def join(pieces):
        if len(pieces) == 1:
            return pieces[0][None]
        shape = (len(pieces),) + pieces[0].shape
        return kernel_call(join_kernel, [(shape, pieces[0].dtype)], "join", list(pieces))[0]

    def together(*values):
        return lax.optimization_barrier(values)

    pieces, first_weight = together(trade_spots(order_history()), pick_head(0))
    first, later = join_layers(pieces)
    x_pieces = trade_spots([after(candidate_rows, first)] * spots)
    crossed = groups == 4
    if crossed:
        near_mask, far_mask = member_masks[1:3]
        far = swap(first, far_mask)
        near = swap(first, near_mask)
        far, near, x_pieces = together(far, near, x_pieces)
        history = [[first, near, far, swap(far, near_mask)]]
    else:
        history = [gather_members(first)]
    x_group = x_pieces + [shift_core(join(x_pieces), s) for s in range(1, cores)]

    scalars = [block_user, block_offset, history_length, candidate_count]
    one_head = (all_rows, head_dim)
    head_outs = [(one_head, jnp.bfloat16), (one_head, jnp.bfloat16), (one_head, jnp.float32)]
    x, *projected = kernel_call(
        functools.partial(begin_kernel, spots, cores, spot_bits, score_scale),
        [((all_rows, model_width), jnp.bfloat16)] + head_outs,
        "begin",
        x_group + [first_weight],
    )

    for layer_index in range(layers):
        last = layer_index + 1 == layers
        outs = [((row_count, head_dim), jnp.bfloat16)] * spots if last else head_outs[:1]
        query, gate, own = projected
        held, split = (), 1
        if crossed:
            parts = 2 if layer_index else 1
            cuts = [spots // parts * part for part in range(parts)]
            held = ((0, 0), (near_mask, 0))
            held += tuple((m, at) for m in (far_mask, near_mask | far_mask) for at in cuts)
            split = 2 + parts + parts // 2
        ready, coming = history[layer_index][:split], history[layer_index][split:]
        operands = scalars + [query, own] + ready
        wide_query, total = kernel_call(
            functools.partial(attend_kernel, spot_bits, masks, held[:split], layer_index),
            [((all_rows, head_dim + LANES), jnp.bfloat16), (one_head, jnp.float32)],
            "attend",
            operands,
            (),
            16,
            [SMEM_SPEC] * 4 + [VMEM_SPEC] * (len(operands) - 4),
        )
        operands = scalars[:3] + [wide_query, total, gate] + coming
        gated = kernel_call(
            functools.partial(finish_kernel, spot_bits, masks, held[split:], layer_index, last),
            outs,
            "finish",
            operands,
            [pltpu.VMEM(one_head, jnp.float32)],
            16,
            [SMEM_SPEC] * 3 + [VMEM_SPEC] * (len(operands) - 3),
        )
        if not last:
            gated = trade_spots(list(gated) * spots)
            next_weight = pick_head(layer_index + 1)
            if crossed:
                whole = after(later[layer_index], far, near)
                far, near = swap(whole, far_mask), swap(whole, near_mask)
                far = halves(after(far, near, gated[1]))
                ahead = swap(far[0], near_mask)
                early, far, next_weight = together(gated[:-1], far, next_weight)
                late, ahead = together(gated[-1:], ahead)
                parts = [(0, early), (spots - 1, late)]
                arrays = [whole, near] + far + [ahead, swap(far[1], near_mask)]
            else:
                arrays = gather_members(later[layer_index])
                parts = [(0, gated)]
            terms = []
            for first_step, heads in parts:
                terms = kernel_call(
                    functools.partial(term_kernel, spot_bits, layer_index, first_step),
                    [
                        (
                            (all_rows, model_width),
                            jnp.bfloat16 if first_step + len(heads) == spots else jnp.float32,
                        )
                    ],
                    "term",
                    heads + [weight_out] + terms,
                )
            terms = terms + [shift_core(terms[0], s) for s in range(1, cores)]
            history.append(arrays)
            x, *projected = kernel_call(
                functools.partial(step_kernel, spots, cores, spot_bits, score_scale),
                [((own_rows, model_width), jnp.bfloat16)] + head_outs,
                "step",
                terms + [x, next_weight],
                [pltpu.VMEM((all_rows, model_width), jnp.bfloat16)],
                12,
            )
        else:
            terms = kernel_call(
                functools.partial(last_term_kernel, spots, cores, spot_bits, layer_index),
                [((own_rows, model_width), jnp.bfloat16)] * cores,
                "last_term",
                trade_spots(gated) + [weight_out],
                [
                    pltpu.VMEM((row_count, spots * head_dim), jnp.bfloat16),
                    pltpu.VMEM((row_count, model_width), jnp.float32),
                ],
            )
            terms = terms[:1] + [shift_core(terms[s], s) for s in range(1, cores)]
            (out,) = kernel_call(
                add_kernel, [((own_rows, model_width), jnp.bfloat16)], "add", [x] + terms
            )
    return out


def solution(mesh):
    placed = (
        P(("users", "cand"), None),
        P(None, None, "cand", None),
        P(None, "cand", None, None),
        P(None, None, "users", "cand", None),
        P(),
        P(),
        P(),
        P(),
    )
    return jax.shard_map(
        body, mesh=mesh, in_specs=placed, out_specs=P(("users", "cand"), None), check_vma=False
    )
```

```python
import functools
import math

import jax
import jax.numpy as jnp
from jax import lax
from jax.experimental import pallas as pl
from jax.experimental.pallas import tpu as pltpu
from jax.sharding import PartitionSpec as P

BLOCK = 128
LANES = 128
FAR = -1e30
MIB = 1024 * 1024

VMEM_SPEC = pl.BlockSpec(memory_space=pltpu.VMEM)
SMEM_SPEC = pl.BlockSpec(memory_space=pltpu.SMEM)


def half_silu(half):
    return half + half * jnp.tanh(half)


def position(spot_bits):
    chip = lax.axis_index("users")
    spot = sum((((chip >> b) & 1) << i for i, b in enumerate(spot_bits)), chip * 0)
    return chip, spot, lax.axis_index("cand")


def order_history_kernel(spot_bits, h_ref, *refs):
    o_refs, pieces = refs[:-1], refs[-1]
    _, spot, _ = position(spot_bits)
    for layer_index in range(h_ref.shape[0]):
        for kind in range(h_ref.shape[1]):
            by_head = jnp.swapaxes(h_ref[layer_index, kind], 0, 1)
            for head in range(h_ref.shape[3]):
                pieces[spot ^ head, layer_index, kind] = by_head[head]
    for step, o_ref in enumerate(o_refs):
        o_ref[...] = pieces[step]


def join_layers_kernel(count, *refs):
    for layer_index, o_ref in enumerate(refs[count:]):
        for at, ref in enumerate(refs[:count]):
            o_ref[at] = ref[layer_index]


def halves_kernel(i_ref, low_ref, high_ref):
    size = low_ref.shape[0]
    low_ref[...] = i_ref[:size]
    high_ref[...] = i_ref[size:]


def join_kernel(*refs):
    o_ref = refs[-1]
    for at, ref in enumerate(refs[:-1]):
        o_ref[at] = ref[...]


def pick_head_kernel(layer_index, spot_bits, w_ref, o_ref, held, sems):
    _, spot, _ = position(spot_bits)
    chunks, rows = held.shape[:2]
    copies = [
        pltpu.make_async_copy(
            w_ref.at[layer_index, pl.ds(at * rows, rows)], held.at[at], sems.at[at]
        )
        for at in range(chunks)
    ]
    for copy in copies:
        copy.start()
    for at, copy in enumerate(copies):
        copy.wait()
        by_head = jnp.swapaxes(held[at], 0, 1)
        for head in range(held.shape[2]):

            @pl.when(spot == head)
            def _(at=at, head=head, by_head=by_head):
                o_ref[at * rows : (at + 1) * rows] = by_head[head]


def project(x_ref, w_ref, q_ref, gate_ref, own_ref, score_scale):
    dim = q_ref.shape[1]

    def part(first):
        w = w_ref[:, first * dim : (first + 2) * dim]
        mixed = jnp.dot(x_ref[...], w, preferred_element_type=jnp.float32)
        return half_silu(mixed * 0.5).astype(jnp.bfloat16)

    tail = part(2)
    query = tail[:, :dim]
    q_ref[...] = query
    score = jnp.sum(
        query.astype(jnp.float32) * tail[:, dim:].astype(jnp.float32), axis=-1, keepdims=True
    )
    weight = half_silu(score * (0.5 * score_scale)).astype(jnp.bfloat16).astype(jnp.float32)
    front = part(0)
    gate_ref[...] = front[:, :dim]
    own_ref[...] = weight * front[:, dim:].astype(jnp.float32)


def begin_kernel(spots, cores, spot_bits, score_scale, *refs):
    _, spot, core_here = position(spot_bits)
    x_refs, (w_ref, x_out, q_ref, gate_ref, own_ref) = refs[:-5], refs[-5:]
    own_rows = x_out.shape[0] // (spots * cores)
    for shift in range(cores):
        core = lax.rem(core_here + (cores - shift), cores)
        for step in range(spots):
            if shift == 0:
                piece = x_refs[step][...]
            else:
                piece = x_refs[spots + shift - 1][step]
            at = ((spot ^ step) * cores + core) * own_rows
            x_out[pl.ds(pl.multiple_of(at, own_rows), own_rows)] = piece
    project(x_out, w_ref, q_ref, gate_ref, own_ref, score_scale)


def gather_heads(gated_refs, spot, wide):
    dim = gated_refs[0].shape[1]
    for step, ref in enumerate(gated_refs):
        at = pl.multiple_of((spot ^ step) * dim, dim)
        wide[:, pl.ds(at, dim)] = ref[...]


def term_kernel(spot_bits, layer_index, first_step, *refs):
    _, spot, _ = position(spot_bits)
    count = len(refs) - 2 - (1 if first_step else 0)
    gated_refs, (weight_ref, *before_refs, o_ref) = refs[:count], refs[count:]
    gated = jnp.concatenate([ref[...] for ref in gated_refs], axis=1)
    width = o_ref.shape[1]
    tile = min(width, 256)
    for first in range(0, width, tile):
        columns = slice(first, first + tile)
        weight = jnp.concatenate(
            [weight_ref[layer_index, spot ^ (first_step + at), :, columns] for at in range(count)],
            axis=0,
        )
        term = jnp.dot(gated, weight, preferred_element_type=jnp.float32)
        if before_refs:
            term = term + before_refs[0][:, columns]
        o_ref[:, columns] = term.astype(o_ref.dtype)


def step_kernel(spots, cores, spot_bits, score_scale, *refs):
    _, spot, core = position(spot_bits)
    term_refs, (x_ref, w_ref, x_own, q_ref, gate_ref, own_ref, x_next) = refs[:cores], refs[cores:]
    total = x_ref[...].astype(jnp.float32)
    for ref in term_refs:
        total = total + ref[...].astype(jnp.float32)
    x_next[...] = total.astype(jnp.bfloat16)
    own_rows = x_own.shape[0]
    at = (spot * cores + core) * own_rows
    x_own[...] = x_next[pl.ds(pl.multiple_of(at, own_rows), own_rows)]
    project(x_next, w_ref, q_ref, gate_ref, own_ref, score_scale)


def last_term_kernel(spots, cores, spot_bits, layer_index, *refs):
    _, spot, core = position(spot_bits)
    gated_refs, (weight_ref, *o_refs, wide, total) = refs[:spots], refs[spots:]
    gather_heads(gated_refs, spot, wide)
    own_rows, width = o_refs[0].shape
    weight = weight_ref[layer_index].reshape(wide.shape[1], width)
    total[...] = jnp.dot(wide[...], weight, preferred_element_type=jnp.float32)
    for shift, o_ref in enumerate(o_refs):
        at = lax.rem(core + shift, cores) * own_rows
        o_ref[...] = total[pl.ds(pl.multiple_of(at, own_rows), own_rows)].astype(jnp.bfloat16)


def add_kernel(*refs):
    total = refs[0][...].astype(jnp.float32)
    for ref in refs[1:-1]:
        total = total + ref[...].astype(jnp.float32)
    refs[-1][...] = total.astype(jnp.bfloat16)


def visit_history(spot_bits, masks, held, layer_index, scalar_refs, history_refs, q_wide, total):
    user_ref, offset_ref, length_ref = scalar_refs
    spot_masks, member_masks, spot_of_chip, row_count = masks
    spots = len(spot_masks)
    dim = total.shape[1]
    scale = 0.5 / math.sqrt(dim)
    chip, _, _ = position(spot_bits)
    spot_part = chip & spot_of_chip
    member_part = chip - spot_part

    def visit(ref, first, count, member, at):
        keys, values = [], []
        for piece in range(count):
            for block in range(ref.shape[2] // BLOCK):
                source = (member | (spot_part ^ spot_masks[at + piece])) * (ref.shape[2] // BLOCK) + block
                owner = user_ref[source]
                limit = length_ref[owner] - offset_ref[source] * BLOCK
                lanes = lax.broadcasted_iota(jnp.int32, (BLOCK, LANES), 1)
                sublanes = lax.broadcasted_iota(jnp.int32, (BLOCK, LANES), 0)
                seen = (lanes == owner) & (sublanes < limit)
                side = jnp.where(seen, 0.0, FAR).astype(jnp.bfloat16)
                at_rows = pl.ds(block * BLOCK, BLOCK)
                keys.append(jnp.concatenate([ref[first + piece, 0, at_rows], side], axis=1))
                values.append(ref[first + piece, 1, at_rows])
        half = lax.dot_general(
            q_wide[...],
            jnp.concatenate(keys, axis=0),
            (((1,), (1,)), ((), ())),
            preferred_element_type=jnp.float32,
        )
        weights = half_silu(half * scale).astype(jnp.bfloat16)
        total[...] += jnp.dot(
            weights, jnp.concatenate(values, axis=0), preferred_element_type=jnp.float32
        )

    if len(history_refs) == len(held):
        for ref, (mask, at) in zip(history_refs, held):
            visit(ref, 0, ref.shape[0], member_part ^ mask, at)
    else:

        @pl.loop(0, len(member_masks))
        def _(turn):
            member = turn * 0
            for i in range((len(member_masks) - 1).bit_length()):
                member = member | (((turn >> i) & 1) * member_masks[1 << i])
            visit(history_refs[0], turn * spots, spots, member, 0)


def attend_kernel(spot_bits, masks, held, layer_index, *refs):
    user_ref, offset_ref, length_ref, count_ref, q_ref, own_ref = refs[:6]
    history_refs, (q_wide, total) = refs[6:-2], refs[-2:]
    spot_masks, member_masks, spot_of_chip, row_count = masks
    spots = len(spot_masks)
    rows = q_ref.shape[0] // spots
    dim = q_ref.shape[1]
    user_count = length_ref.shape[0]
    chip, _, _ = position(spot_bits)
    member_part = chip - (chip & spot_of_chip)
    lane = lax.broadcasted_iota(jnp.int32, (1, LANES), 1)
    starts = jnp.zeros((1, LANES), jnp.int32)
    ends = jnp.zeros((1, LANES), jnp.int32)
    running = jnp.int32(0)
    for user in range(user_count):
        starts = jnp.where(lane == user, running, starts)
        running = running + count_ref[user]
        ends = jnp.where(lane == user, running, ends)
    q_wide[:, :dim] = q_ref[...]
    for at in range(spots):
        first = (member_part | spot_masks[at]) * row_count
        index = first + lax.broadcasted_iota(jnp.int32, (rows, LANES), 0)
        mine = (index >= starts) & (index < ends)
        q_wide[at * rows : (at + 1) * rows, dim:] = jnp.where(mine, 1.0, 0.0).astype(
            jnp.bfloat16
        )
    total[...] = own_ref[...]
    visit_history(
        spot_bits,
        masks,
        held,
        layer_index,
        (user_ref, offset_ref, length_ref),
        history_refs,
        q_wide,
        total,
    )


def finish_kernel(spot_bits, masks, held, layer_index, last, *refs):
    scalar_refs, (q_wide, before_ref, gate_ref), refs = refs[:3], refs[3:6], refs[6:]
    spots = len(masks[0])
    outs = spots if last else 1
    history_refs, o_refs, total = refs[: -outs - 1], refs[-outs - 1 : -1], refs[-1]
    rows = before_ref.shape[0] // spots
    _, spot, _ = position(spot_bits)
    total[...] = before_ref[...]
    if history_refs:
        visit_history(
            spot_bits, masks, held, layer_index, scalar_refs, history_refs, q_wide, total
        )
    full = total[...]
    centred = full - jnp.mean(full, axis=-1, keepdims=True)
    variance = jnp.mean(centred * centred, axis=-1, keepdims=True)
    gated = centred * lax.rsqrt(variance + 1e-05) * gate_ref[...].astype(jnp.float32)
    if not last:
        o_refs[0][...] = gated.astype(jnp.bfloat16)
        return
    total[...] = gated
    for step in range(spots):
        at_rows = pl.ds(pl.multiple_of((spot ^ step) * rows, rows), rows)
        o_refs[step][...] = total[at_rows].astype(jnp.bfloat16)


def body(
    candidate_rows,
    weight_in,
    weight_out,
    history_cache,
    block_user,
    block_offset,
    history_length,
    candidate_count,
):
    own_rows, model_width = candidate_rows.shape
    layers, model_again, heads_here, packed = weight_in.shape
    head_dim = packed // 4
    local_rows = history_cache.shape[2]
    cores = lax.axis_size("cand")
    chips = lax.axis_size("users")
    spots = heads_here
    groups = chips // spots
    row_count = own_rows * cores
    all_rows = row_count * spots
    score_scale = 1.0 / math.sqrt(head_dim)

    bits = list(range(chips.bit_length() - 1))
    spot_bits = sorted((bits[::2] + bits[1::2])[: spots.bit_length() - 1])
    member_bits = [b for b in bits if b not in spot_bits]

    def mask_of(number, places):
        return sum(((number >> i) & 1) << b for i, b in enumerate(places))

    def swap(value, mask):
        return lax.ppermute(value, "users", [(u, u ^ mask) for u in range(chips)])

    def trade_spots(values, diagonal_first=True):
        steps = range(1, spots)
        moved = {0: values[0]}
        for m in reversed(steps) if diagonal_first else steps:
            moved[m] = swap(values[m], mask_of(m, spot_bits))
        return [moved[m] for m in range(spots)]

    def gather_spots(value):
        found = [value]
        for bit in reversed(range(len(spot_bits))):
            mask = 1 << spot_bits[bit]
            found = [(v, swap(v, mask)) for v in found]
            found = [v for v, _ in found] + [w for _, w in found]
        order = [0]
        for bit in reversed(range(len(spot_bits))):
            order = order + [o | (1 << bit) for o in order]
        return [found[order.index(m)] for m in range(spots)]

    def shift_core(value, step):
        pairs = [(c, (c + step) % cores) for c in range(cores)]
        return lax.ppermute(value, "cand", pairs)

    spot_masks = [mask_of(m, spot_bits) for m in range(spots)]
    member_masks = [mask_of(m, member_bits) for m in range(groups)]

    masks = (spot_masks, member_masks, spot_masks[-1], row_count)

    def gather_members(pieces):
        if groups <= 2:
            return [pieces] + [swap(pieces, mask) for mask in member_masks[1:]]
        chips_of = [[mask_of(s, spot_bits) | m for m in member_masks] for s in range(spots)]
        return [
            lax.all_gather(pieces, "users", axis=0, axis_index_groups=chips_of, tiled=True)
        ]

    def after(value, *others):
        return lax.optimization_barrier((value,) + others)[0]

    def kernel_call(kernel, outs, name, operands, scratch=(), limit=8, specs=None):
        results = pl.pallas_call(
            kernel,
            out_shape=[jax.ShapeDtypeStruct(*out) for out in outs],
            in_specs=specs or [VMEM_SPEC] * len(operands),
            out_specs=[VMEM_SPEC] * len(outs),
            scratch_shapes=scratch,
            compiler_params=pltpu.CompilerParams(vmem_limit_bytes=limit * MIB),
            name=name,
        )(*operands)
        return list(results)

    def pick_head(layer_index):
        rows = min(model_width, 128)
        chunks = model_width // rows
        return kernel_call(
            functools.partial(pick_head_kernel, layer_index, spot_bits),
            [((model_width, packed), weight_in.dtype)],
            "pick_head",
            [weight_in],
            [
                pltpu.VMEM((chunks, rows, heads_here, packed), weight_in.dtype),
                pltpu.SemaphoreType.DMA((chunks,)),
            ],
            51,
            [pl.BlockSpec(memory_space=pl.ANY)],
        )[0]

    def order_history():
        shape = (layers, 2, local_rows, head_dim)
        return kernel_call(
            functools.partial(order_history_kernel, spot_bits),
            [(shape, jnp.bfloat16)] * spots,
            "order_history",
            [history_cache],
            [pltpu.VMEM((spots,) + shape, jnp.bfloat16)],
            4,
        )

    def join_layers(pieces):
        shape = (spots, 2, local_rows, head_dim)
        first, *later = kernel_call(
            functools.partial(join_layers_kernel, spots),
            [(shape, jnp.bfloat16)] * layers,
            "join_layers",
            list(pieces),
        )
        return first, later

    def halves(pieces):
        shape = (pieces.shape[0] // 2,) + pieces.shape[1:]
        return kernel_call(halves_kernel, [(shape, pieces.dtype)] * 2, "halves", [pieces])

    def join(pieces):
        if len(pieces) == 1:
            return pieces[0][None]
        shape = (len(pieces),) + pieces[0].shape
        return kernel_call(join_kernel, [(shape, pieces[0].dtype)], "join", list(pieces))[0]

    def together(*values):
        return lax.optimization_barrier(values)

    pieces, first_weight = together(trade_spots(order_history()), pick_head(0))
    first, later = join_layers(pieces)
    x_pieces = trade_spots([after(candidate_rows, first)] * spots)
    crossed = groups == 4
    if crossed:
        near_mask, far_mask = member_masks[1:3]
        far = swap(first, far_mask)
        near = swap(first, near_mask)
        far, near, x_pieces = together(far, near, x_pieces)
        history = [[first, near, far, swap(far, near_mask)]]
    else:
        history = [gather_members(first)]
    x_group = x_pieces + [shift_core(join(x_pieces), s) for s in range(1, cores)]

    scalars = [block_user, block_offset, history_length, candidate_count]
    one_head = (all_rows, head_dim)
    head_outs = [(one_head, jnp.bfloat16), (one_head, jnp.bfloat16), (one_head, jnp.float32)]
    x, *projected = kernel_call(
        functools.partial(begin_kernel, spots, cores, spot_bits, score_scale),
        [((all_rows, model_width), jnp.bfloat16)] + head_outs,
        "begin",
        x_group + [first_weight],
    )

    for layer_index in range(layers):
        last = layer_index + 1 == layers
        outs = [((row_count, head_dim), jnp.bfloat16)] * spots if last else head_outs[:1]
        query, gate, own = projected
        held, split = (), 1
        if crossed:
            parts = 2 if layer_index else 1
            cuts = [spots // parts * part for part in range(parts)]
            held = ((0, 0), (near_mask, 0))
            held += tuple((m, at) for m in (far_mask, near_mask | far_mask) for at in cuts)
            split = 2 + parts + parts // 2
        ready, coming = history[layer_index][:split], history[layer_index][split:]
        operands = scalars + [query, own] + ready
        wide_query, total = kernel_call(
            functools.partial(attend_kernel, spot_bits, masks, held[:split], layer_index),
            [((all_rows, head_dim + LANES), jnp.bfloat16), (one_head, jnp.float32)],
            "attend",
            operands,
            (),
            16,
            [SMEM_SPEC] * 4 + [VMEM_SPEC] * (len(operands) - 4),
        )
        operands = scalars[:3] + [wide_query, total, gate] + coming
        gated = kernel_call(
            functools.partial(finish_kernel, spot_bits, masks, held[split:], layer_index, last),
            outs,
            "finish",
            operands,
            [pltpu.VMEM(one_head, jnp.float32)],
            16,
            [SMEM_SPEC] * 3 + [VMEM_SPEC] * (len(operands) - 3),
        )
        if not last:
            gated = trade_spots(list(gated) * spots, False)
            next_weight = pick_head(layer_index + 1)
            if crossed:
                whole = after(later[layer_index], far, near)
                far, near = swap(whole, far_mask), swap(whole, near_mask)
                far = halves(after(far, near, gated[1]))
                ahead = swap(far[0], near_mask)
                early, far, next_weight = together(gated[:-1], far, next_weight)
                late, ahead = together(gated[-1:], ahead)
                parts = [(0, early), (spots - 1, late)]
                arrays = [whole, near] + far + [ahead, swap(far[1], near_mask)]
            else:
                arrays = gather_members(later[layer_index])
                parts = [(0, gated)]
            terms = []
            for first_step, heads in parts:
                terms = kernel_call(
                    functools.partial(term_kernel, spot_bits, layer_index, first_step),
                    [
                        (
                            (all_rows, model_width),
                            jnp.bfloat16 if first_step + len(heads) == spots else jnp.float32,
                        )
                    ],
                    "term",
                    heads + [weight_out] + terms,
                )
            terms = terms + [shift_core(terms[0], s) for s in range(1, cores)]
            history.append(arrays)
            x, *projected = kernel_call(
                functools.partial(step_kernel, spots, cores, spot_bits, score_scale),
                [((own_rows, model_width), jnp.bfloat16)] + head_outs,
                "step",
                terms + [x, next_weight],
                [pltpu.VMEM((all_rows, model_width), jnp.bfloat16)],
                12,
            )
        else:
            terms = kernel_call(
                functools.partial(last_term_kernel, spots, cores, spot_bits, layer_index),
                [((own_rows, model_width), jnp.bfloat16)] * cores,
                "last_term",
                trade_spots(gated) + [weight_out],
                [
                    pltpu.VMEM((row_count, spots * head_dim), jnp.bfloat16),
                    pltpu.VMEM((row_count, model_width), jnp.float32),
                ],
            )
            terms = terms[:1] + [shift_core(terms[s], s) for s in range(1, cores)]
            (out,) = kernel_call(
                add_kernel, [((own_rows, model_width), jnp.bfloat16)], "add", [x] + terms
            )
    return out


def solution(mesh):
    placed = (
        P(("users", "cand"), None),
        P(None, None, "cand", None),
        P(None, "cand", None, None),
        P(None, None, "users", "cand", None),
        P(),
        P(),
        P(),
        P(),
    )
    return jax.shard_map(
        body, mesh=mesh, in_specs=placed, out_specs=P(("users", "cand"), None), check_vma=False
    )
```

```python
import functools
import math

import jax
import jax.numpy as jnp
from jax import lax
from jax.experimental import pallas as pl
from jax.experimental.pallas import tpu as pltpu
from jax.sharding import PartitionSpec as P

BLOCK = 128
LANES = 128
FAR = -1e30
MIB = 1024 * 1024

VMEM_SPEC = pl.BlockSpec(memory_space=pltpu.VMEM)
SMEM_SPEC = pl.BlockSpec(memory_space=pltpu.SMEM)


def half_silu(half):
    return half + half * jnp.tanh(half)


def position(spot_bits):
    chip = lax.axis_index("users")
    spot = sum((((chip >> b) & 1) << i for i, b in enumerate(spot_bits)), chip * 0)
    return chip, spot, lax.axis_index("cand")


def order_history_kernel(spot_bits, h_ref, *refs):
    o_refs, pieces = refs[:-1], refs[-1]
    _, spot, _ = position(spot_bits)
    for layer_index in range(h_ref.shape[0]):
        for kind in range(h_ref.shape[1]):
            by_head = jnp.swapaxes(h_ref[layer_index, kind], 0, 1)
            for head in range(h_ref.shape[3]):
                pieces[spot ^ head, layer_index, kind] = by_head[head]
    for step, o_ref in enumerate(o_refs):
        o_ref[...] = pieces[step]


def join_layers_kernel(count, *refs):
    for layer_index, o_ref in enumerate(refs[count:]):
        for at, ref in enumerate(refs[:count]):
            o_ref[at] = ref[layer_index]


def halves_kernel(i_ref, low_ref, high_ref):
    size = low_ref.shape[0]
    low_ref[...] = i_ref[:size]
    high_ref[...] = i_ref[size:]


def join_kernel(*refs):
    o_ref = refs[-1]
    for at, ref in enumerate(refs[:-1]):
        o_ref[at] = ref[...]


def pick_head_kernel(layer_index, spot_bits, w_ref, o_ref, held, sems):
    _, spot, _ = position(spot_bits)
    chunks, rows = held.shape[:2]
    copies = [
        pltpu.make_async_copy(
            w_ref.at[layer_index, pl.ds(at * rows, rows)], held.at[at], sems.at[at]
        )
        for at in range(chunks)
    ]
    for copy in copies:
        copy.start()
    for at, copy in enumerate(copies):
        copy.wait()
        by_head = jnp.swapaxes(held[at], 0, 1)
        for head in range(held.shape[2]):

            @pl.when(spot == head)
            def _(at=at, head=head, by_head=by_head):
                o_ref[at * rows : (at + 1) * rows] = by_head[head]


def project(x_ref, w_ref, q_ref, gate_ref, own_ref, score_scale):
    dim = q_ref.shape[1]

    def part(first):
        w = w_ref[:, first * dim : (first + 2) * dim]
        mixed = jnp.dot(x_ref[...], w, preferred_element_type=jnp.float32)
        return half_silu(mixed * 0.5).astype(jnp.bfloat16)

    tail = part(2)
    query = tail[:, :dim]
    q_ref[...] = query
    score = jnp.sum(
        query.astype(jnp.float32) * tail[:, dim:].astype(jnp.float32), axis=-1, keepdims=True
    )
    weight = half_silu(score * (0.5 * score_scale)).astype(jnp.bfloat16).astype(jnp.float32)
    front = part(0)
    gate_ref[...] = front[:, :dim]
    own_ref[...] = weight * front[:, dim:].astype(jnp.float32)


def begin_kernel(spots, cores, spot_bits, score_scale, *refs):
    _, spot, core_here = position(spot_bits)
    x_refs, (w_ref, x_out, q_ref, gate_ref, own_ref) = refs[:-5], refs[-5:]
    own_rows = x_out.shape[0] // (spots * cores)
    for shift in range(cores):
        core = lax.rem(core_here + (cores - shift), cores)
        for step in range(spots):
            if shift == 0:
                piece = x_refs[step][...]
            else:
                piece = x_refs[spots + shift - 1][step]
            at = ((spot ^ step) * cores + core) * own_rows
            x_out[pl.ds(pl.multiple_of(at, own_rows), own_rows)] = piece
    project(x_out, w_ref, q_ref, gate_ref, own_ref, score_scale)


def gather_heads(gated_refs, spot, wide):
    dim = gated_refs[0].shape[1]
    for step, ref in enumerate(gated_refs):
        at = pl.multiple_of((spot ^ step) * dim, dim)
        wide[:, pl.ds(at, dim)] = ref[...]


def term_kernel(spot_bits, layer_index, first_step, *refs):
    _, spot, _ = position(spot_bits)
    count = len(refs) - 2 - (1 if first_step else 0)
    gated_refs, (weight_ref, *before_refs, o_ref) = refs[:count], refs[count:]
    gated = jnp.concatenate([ref[...] for ref in gated_refs], axis=1)
    width = o_ref.shape[1]
    tile = min(width, 256)
    for first in range(0, width, tile):
        columns = slice(first, first + tile)
        weight = jnp.concatenate(
            [weight_ref[layer_index, spot ^ (first_step + at), :, columns] for at in range(count)],
            axis=0,
        )
        term = jnp.dot(gated, weight, preferred_element_type=jnp.float32)
        if before_refs:
            term = term + before_refs[0][:, columns]
        o_ref[:, columns] = term.astype(o_ref.dtype)


def step_kernel(spots, cores, spot_bits, score_scale, *refs):
    _, spot, core = position(spot_bits)
    term_refs, (x_ref, w_ref, x_own, q_ref, gate_ref, own_ref, x_next) = refs[:cores], refs[cores:]
    total = x_ref[...].astype(jnp.float32)
    for ref in term_refs:
        total = total + ref[...].astype(jnp.float32)
    x_next[...] = total.astype(jnp.bfloat16)
    own_rows = x_own.shape[0]
    at = (spot * cores + core) * own_rows
    x_own[...] = x_next[pl.ds(pl.multiple_of(at, own_rows), own_rows)]
    project(x_next, w_ref, q_ref, gate_ref, own_ref, score_scale)


def last_term_kernel(spots, cores, spot_bits, layer_index, *refs):
    _, spot, core = position(spot_bits)
    gated_refs, (weight_ref, *o_refs, wide, total) = refs[:spots], refs[spots:]
    gather_heads(gated_refs, spot, wide)
    own_rows, width = o_refs[0].shape
    weight = weight_ref[layer_index].reshape(wide.shape[1], width)
    total[...] = jnp.dot(wide[...], weight, preferred_element_type=jnp.float32)
    for shift, o_ref in enumerate(o_refs):
        at = lax.rem(core + shift, cores) * own_rows
        o_ref[...] = total[pl.ds(pl.multiple_of(at, own_rows), own_rows)].astype(jnp.bfloat16)


def add_kernel(*refs):
    total = refs[0][...].astype(jnp.float32)
    for ref in refs[1:-1]:
        total = total + ref[...].astype(jnp.float32)
    refs[-1][...] = total.astype(jnp.bfloat16)


def visit_history(spot_bits, masks, held, layer_index, scalar_refs, history_refs, q_wide, total):
    user_ref, offset_ref, length_ref = scalar_refs
    spot_masks, member_masks, spot_of_chip, row_count = masks
    spots = len(spot_masks)
    dim = total.shape[1]
    scale = 0.5 / math.sqrt(dim)
    chip, _, _ = position(spot_bits)
    spot_part = chip & spot_of_chip
    member_part = chip - spot_part

    def visit(ref, first, count, member, at):
        keys, values = [], []
        for piece in range(count):
            for block in range(ref.shape[2] // BLOCK):
                source = (member | (spot_part ^ spot_masks[at + piece])) * (ref.shape[2] // BLOCK) + block
                owner = user_ref[source]
                limit = length_ref[owner] - offset_ref[source] * BLOCK
                lanes = lax.broadcasted_iota(jnp.int32, (BLOCK, LANES), 1)
                sublanes = lax.broadcasted_iota(jnp.int32, (BLOCK, LANES), 0)
                seen = (lanes == owner) & (sublanes < limit)
                side = jnp.where(seen, 0.0, FAR).astype(jnp.bfloat16)
                at_rows = pl.ds(block * BLOCK, BLOCK)
                keys.append(jnp.concatenate([ref[first + piece, 0, at_rows], side], axis=1))
                values.append(ref[first + piece, 1, at_rows])
        half = lax.dot_general(
            q_wide[...],
            jnp.concatenate(keys, axis=0),
            (((1,), (1,)), ((), ())),
            preferred_element_type=jnp.float32,
        )
        weights = half_silu(half * scale).astype(jnp.bfloat16)
        total[...] += jnp.dot(
            weights, jnp.concatenate(values, axis=0), preferred_element_type=jnp.float32
        )

    if len(history_refs) == len(held):
        for ref, (mask, at) in zip(history_refs, held):
            visit(ref, 0, ref.shape[0], member_part ^ mask, at)
    else:

        @pl.loop(0, len(member_masks))
        def _(turn):
            member = turn * 0
            for i in range((len(member_masks) - 1).bit_length()):
                member = member | (((turn >> i) & 1) * member_masks[1 << i])
            visit(history_refs[0], turn * spots, spots, member, 0)


def attend_kernel(spot_bits, masks, held, layer_index, *refs):
    user_ref, offset_ref, length_ref, count_ref, q_ref, own_ref = refs[:6]
    history_refs, (q_wide, total) = refs[6:-2], refs[-2:]
    spot_masks, member_masks, spot_of_chip, row_count = masks
    spots = len(spot_masks)
    rows = q_ref.shape[0] // spots
    dim = q_ref.shape[1]
    user_count = length_ref.shape[0]
    chip, _, _ = position(spot_bits)
    member_part = chip - (chip & spot_of_chip)
    lane = lax.broadcasted_iota(jnp.int32, (1, LANES), 1)
    starts = jnp.zeros((1, LANES), jnp.int32)
    ends = jnp.zeros((1, LANES), jnp.int32)
    running = jnp.int32(0)
    for user in range(user_count):
        starts = jnp.where(lane == user, running, starts)
        running = running + count_ref[user]
        ends = jnp.where(lane == user, running, ends)
    q_wide[:, :dim] = q_ref[...]
    for at in range(spots):
        first = (member_part | spot_masks[at]) * row_count
        index = first + lax.broadcasted_iota(jnp.int32, (rows, LANES), 0)
        mine = (index >= starts) & (index < ends)
        q_wide[at * rows : (at + 1) * rows, dim:] = jnp.where(mine, 1.0, 0.0).astype(
            jnp.bfloat16
        )
    total[...] = own_ref[...]
    visit_history(
        spot_bits,
        masks,
        held,
        layer_index,
        (user_ref, offset_ref, length_ref),
        history_refs,
        q_wide,
        total,
    )


def finish_kernel(spot_bits, masks, held, layer_index, last, *refs):
    scalar_refs, (q_wide, before_ref, gate_ref), refs = refs[:3], refs[3:6], refs[6:]
    spots = len(masks[0])
    outs = spots if last else 1
    history_refs, o_refs, total = refs[: -outs - 1], refs[-outs - 1 : -1], refs[-1]
    rows = before_ref.shape[0] // spots
    _, spot, _ = position(spot_bits)
    total[...] = before_ref[...]
    if history_refs:
        visit_history(
            spot_bits, masks, held, layer_index, scalar_refs, history_refs, q_wide, total
        )
    full = total[...]
    centred = full - jnp.mean(full, axis=-1, keepdims=True)
    variance = jnp.mean(centred * centred, axis=-1, keepdims=True)
    gated = centred * lax.rsqrt(variance + 1e-05) * gate_ref[...].astype(jnp.float32)
    if not last:
        o_refs[0][...] = gated.astype(jnp.bfloat16)
        return
    total[...] = gated
    for step in range(spots):
        at_rows = pl.ds(pl.multiple_of((spot ^ step) * rows, rows), rows)
        o_refs[step][...] = total[at_rows].astype(jnp.bfloat16)


def body(
    candidate_rows,
    weight_in,
    weight_out,
    history_cache,
    block_user,
    block_offset,
    history_length,
    candidate_count,
):
    own_rows, model_width = candidate_rows.shape
    layers, model_again, heads_here, packed = weight_in.shape
    head_dim = packed // 4
    local_rows = history_cache.shape[2]
    cores = lax.axis_size("cand")
    chips = lax.axis_size("users")
    spots = heads_here
    groups = chips // spots
    row_count = own_rows * cores
    all_rows = row_count * spots
    score_scale = 1.0 / math.sqrt(head_dim)

    bits = list(range(chips.bit_length() - 1))
    spot_bits = sorted((bits[::2] + bits[1::2])[: spots.bit_length() - 1])
    member_bits = [b for b in bits if b not in spot_bits]

    def mask_of(number, places):
        return sum(((number >> i) & 1) << b for i, b in enumerate(places))

    def swap(value, mask):
        return lax.ppermute(value, "users", [(u, u ^ mask) for u in range(chips)])

    def trade_spots(values, diagonal_first=True):
        steps = range(1, spots)
        moved = {0: values[0]}
        for m in reversed(steps) if diagonal_first else steps:
            moved[m] = swap(values[m], mask_of(m, spot_bits))
        return [moved[m] for m in range(spots)]

    def gather_spots(value):
        found = [value]
        for bit in reversed(range(len(spot_bits))):
            mask = 1 << spot_bits[bit]
            found = [(v, swap(v, mask)) for v in found]
            found = [v for v, _ in found] + [w for _, w in found]
        order = [0]
        for bit in reversed(range(len(spot_bits))):
            order = order + [o | (1 << bit) for o in order]
        return [found[order.index(m)] for m in range(spots)]

    def shift_core(value, step):
        pairs = [(c, (c + step) % cores) for c in range(cores)]
        return lax.ppermute(value, "cand", pairs)

    spot_masks = [mask_of(m, spot_bits) for m in range(spots)]
    member_masks = [mask_of(m, member_bits) for m in range(groups)]

    masks = (spot_masks, member_masks, spot_masks[-1], row_count)

    def gather_members(pieces):
        if groups <= 2:
            return [pieces] + [swap(pieces, mask) for mask in member_masks[1:]]
        chips_of = [[mask_of(s, spot_bits) | m for m in member_masks] for s in range(spots)]
        return [
            lax.all_gather(pieces, "users", axis=0, axis_index_groups=chips_of, tiled=True)
        ]

    def after(value, *others):
        return lax.optimization_barrier((value,) + others)[0]

    def kernel_call(kernel, outs, name, operands, scratch=(), limit=8, specs=None):
        results = pl.pallas_call(
            kernel,
            out_shape=[jax.ShapeDtypeStruct(*out) for out in outs],
            in_specs=specs or [VMEM_SPEC] * len(operands),
            out_specs=[VMEM_SPEC] * len(outs),
            scratch_shapes=scratch,
            compiler_params=pltpu.CompilerParams(vmem_limit_bytes=limit * MIB),
            name=name,
        )(*operands)
        return list(results)

    def pick_head(layer_index):
        rows = min(model_width, 128)
        chunks = model_width // rows
        return kernel_call(
            functools.partial(pick_head_kernel, layer_index, spot_bits),
            [((model_width, packed), weight_in.dtype)],
            "pick_head",
            [weight_in],
            [
                pltpu.VMEM((chunks, rows, heads_here, packed), weight_in.dtype),
                pltpu.SemaphoreType.DMA((chunks,)),
            ],
            51,
            [pl.BlockSpec(memory_space=pl.ANY)],
        )[0]

    def order_history():
        shape = (layers, 2, local_rows, head_dim)
        return kernel_call(
            functools.partial(order_history_kernel, spot_bits),
            [(shape, jnp.bfloat16)] * spots,
            "order_history",
            [history_cache],
            [pltpu.VMEM((spots,) + shape, jnp.bfloat16)],
            4,
        )

    def join_layers(pieces):
        shape = (spots, 2, local_rows, head_dim)
        first, *later = kernel_call(
            functools.partial(join_layers_kernel, spots),
            [(shape, jnp.bfloat16)] * layers,
            "join_layers",
            list(pieces),
        )
        return first, later

    def halves(pieces):
        shape = (pieces.shape[0] // 2,) + pieces.shape[1:]
        return kernel_call(halves_kernel, [(shape, pieces.dtype)] * 2, "halves", [pieces])

    def join(pieces):
        if len(pieces) == 1:
            return pieces[0][None]
        shape = (len(pieces),) + pieces[0].shape
        return kernel_call(join_kernel, [(shape, pieces[0].dtype)], "join", list(pieces))[0]

    def together(*values):
        return lax.optimization_barrier(values)

    pieces, first_weight = together(trade_spots(order_history()), pick_head(0))
    first, later = join_layers(pieces)
    x_pieces = trade_spots([after(candidate_rows, first)] * spots)
    crossed = groups == 4
    if crossed:
        near_mask, far_mask = member_masks[1:3]
        far = swap(first, far_mask)
        near = swap(first, near_mask)
        far, near = together(far, near)
        onward = swap(far, near_mask)
        x_pieces[1:] = [after(piece, far) for piece in x_pieces[1:]]
        history = [[first, near, far, onward]]
    else:
        history = [gather_members(first)]
    x_group = x_pieces + [shift_core(join(x_pieces), s) for s in range(1, cores)]

    scalars = [block_user, block_offset, history_length, candidate_count]
    one_head = (all_rows, head_dim)
    head_outs = [(one_head, jnp.bfloat16), (one_head, jnp.bfloat16), (one_head, jnp.float32)]
    x, *projected = kernel_call(
        functools.partial(begin_kernel, spots, cores, spot_bits, score_scale),
        [((all_rows, model_width), jnp.bfloat16)] + head_outs,
        "begin",
        x_group + [first_weight],
    )

    for layer_index in range(layers):
        last = layer_index + 1 == layers
        outs = [((row_count, head_dim), jnp.bfloat16)] * spots if last else head_outs[:1]
        query, gate, own = projected
        held, split = (), 1
        if crossed:
            parts = 2 if layer_index else 1
            cuts = [spots // parts * part for part in range(parts)]
            held = ((0, 0), (near_mask, 0))
            held += tuple((m, at) for m in (far_mask, near_mask | far_mask) for at in cuts)
            split = 2 + parts + parts // 2
        ready, coming = history[layer_index][:split], history[layer_index][split:]
        operands = scalars + [query, own] + ready
        wide_query, total = kernel_call(
            functools.partial(attend_kernel, spot_bits, masks, held[:split], layer_index),
            [((all_rows, head_dim + LANES), jnp.bfloat16), (one_head, jnp.float32)],
            "attend",
            operands,
            (),
            16,
            [SMEM_SPEC] * 4 + [VMEM_SPEC] * (len(operands) - 4),
        )
        operands = scalars[:3] + [wide_query, total, gate] + coming
        gated = kernel_call(
            functools.partial(finish_kernel, spot_bits, masks, held[split:], layer_index, last),
            outs,
            "finish",
            operands,
            [pltpu.VMEM(one_head, jnp.float32)],
            16,
            [SMEM_SPEC] * 3 + [VMEM_SPEC] * (len(operands) - 3),
        )
        if not last:
            gated = trade_spots(list(gated) * spots, False)
            next_weight = pick_head(layer_index + 1)
            if crossed:
                whole = after(later[layer_index], far, near)
                far, near = swap(whole, far_mask), swap(whole, near_mask)
                far = halves(after(far, near, gated[1]))
                ahead = swap(far[0], near_mask)
                early, far, next_weight = together(gated[:-1], far, next_weight)
                late, ahead = together(gated[-1:], ahead)
                parts = [(0, early), (spots - 1, late)]
                arrays = [whole, near] + far + [ahead, swap(far[1], near_mask)]
            else:
                arrays = gather_members(later[layer_index])
                parts = [(0, gated)]
            terms = []
            for first_step, heads in parts:
                terms = kernel_call(
                    functools.partial(term_kernel, spot_bits, layer_index, first_step),
                    [
                        (
                            (all_rows, model_width),
                            jnp.bfloat16 if first_step + len(heads) == spots else jnp.float32,
                        )
                    ],
                    "term",
                    heads + [weight_out] + terms,
                )
            terms = terms + [shift_core(terms[0], s) for s in range(1, cores)]
            history.append(arrays)
            x, *projected = kernel_call(
                functools.partial(step_kernel, spots, cores, spot_bits, score_scale),
                [((own_rows, model_width), jnp.bfloat16)] + head_outs,
                "step",
                terms + [x, next_weight],
                [pltpu.VMEM((all_rows, model_width), jnp.bfloat16)],
                12,
            )
        else:
            terms = kernel_call(
                functools.partial(last_term_kernel, spots, cores, spot_bits, layer_index),
                [((own_rows, model_width), jnp.bfloat16)] * cores,
                "last_term",
                trade_spots(gated) + [weight_out],
                [
                    pltpu.VMEM((row_count, spots * head_dim), jnp.bfloat16),
                    pltpu.VMEM((row_count, model_width), jnp.float32),
                ],
            )
            terms = terms[:1] + [shift_core(terms[s], s) for s in range(1, cores)]
            (out,) = kernel_call(
                add_kernel, [((own_rows, model_width), jnp.bfloat16)], "add", [x] + terms
            )
    return out


def solution(mesh):
    placed = (
        P(("users", "cand"), None),
        P(None, None, "cand", None),
        P(None, "cand", None, None),
        P(None, None, "users", "cand", None),
        P(),
        P(),
        P(),
        P(),
    )
    return jax.shard_map(
        body, mesh=mesh, in_specs=placed, out_specs=P(("users", "cand"), None), check_vma=False
    )
```

```python
import functools
import math

import jax
import jax.numpy as jnp
from jax import lax
from jax.experimental import pallas as pl
from jax.experimental.pallas import tpu as pltpu
from jax.sharding import PartitionSpec as P

BLOCK = 128
LANES = 128
FAR = -1e30
MIB = 1024 * 1024

VMEM_SPEC = pl.BlockSpec(memory_space=pltpu.VMEM)
SMEM_SPEC = pl.BlockSpec(memory_space=pltpu.SMEM)


def half_silu(half):
    return half + half * jnp.tanh(half)


def position(spot_bits):
    chip = lax.axis_index("users")
    spot = sum((((chip >> b) & 1) << i for i, b in enumerate(spot_bits)), chip * 0)
    return chip, spot, lax.axis_index("cand")


def order_history_kernel(spot_bits, h_ref, *refs):
    o_refs, pieces = refs[:-1], refs[-1]
    _, spot, _ = position(spot_bits)
    for layer_index in range(h_ref.shape[0]):
        for kind in range(h_ref.shape[1]):
            by_head = jnp.swapaxes(h_ref[layer_index, kind], 0, 1)
            for head in range(h_ref.shape[3]):
                pieces[spot ^ head, layer_index, kind] = by_head[head]
    for step, o_ref in enumerate(o_refs):
        o_ref[...] = pieces[step]


def join_layers_kernel(count, *refs):
    for layer_index, o_ref in enumerate(refs[count:]):
        for at, ref in enumerate(refs[:count]):
            o_ref[at] = ref[layer_index]


def halves_kernel(i_ref, low_ref, high_ref):
    size = low_ref.shape[0]
    low_ref[...] = i_ref[:size]
    high_ref[...] = i_ref[size:]


def join_kernel(*refs):
    o_ref = refs[-1]
    for at, ref in enumerate(refs[:-1]):
        o_ref[at] = ref[...]


def pick_head_kernel(layer_index, spot_bits, w_ref, o_ref, held, sems):
    _, spot, _ = position(spot_bits)
    chunks, rows = held.shape[:2]
    copies = [
        pltpu.make_async_copy(
            w_ref.at[layer_index, pl.ds(at * rows, rows)], held.at[at], sems.at[at]
        )
        for at in range(chunks)
    ]
    for copy in copies:
        copy.start()
    for at, copy in enumerate(copies):
        copy.wait()
        by_head = jnp.swapaxes(held[at], 0, 1)
        for head in range(held.shape[2]):

            @pl.when(spot == head)
            def _(at=at, head=head, by_head=by_head):
                o_ref[at * rows : (at + 1) * rows] = by_head[head]


def project(x_ref, w_ref, q_ref, gate_ref, own_ref, score_scale):
    dim = q_ref.shape[1]

    def part(first):
        w = w_ref[:, first * dim : (first + 2) * dim]
        mixed = jnp.dot(x_ref[...], w, preferred_element_type=jnp.float32)
        return half_silu(mixed * 0.5).astype(jnp.bfloat16)

    tail = part(2)
    query = tail[:, :dim]
    q_ref[...] = query
    score = jnp.sum(
        query.astype(jnp.float32) * tail[:, dim:].astype(jnp.float32), axis=-1, keepdims=True
    )
    weight = half_silu(score * (0.5 * score_scale)).astype(jnp.bfloat16).astype(jnp.float32)
    front = part(0)
    gate_ref[...] = front[:, :dim]
    own_ref[...] = weight * front[:, dim:].astype(jnp.float32)


def begin_kernel(spots, cores, spot_bits, score_scale, *refs):
    _, spot, core_here = position(spot_bits)
    x_refs, (w_ref, x_out, q_ref, gate_ref, own_ref) = refs[:-5], refs[-5:]
    own_rows = x_out.shape[0] // (spots * cores)
    for shift in range(cores):
        core = lax.rem(core_here + (cores - shift), cores)
        for step in range(spots):
            piece = x_refs[shift * spots + step][...]
            at = ((spot ^ step) * cores + core) * own_rows
            x_out[pl.ds(pl.multiple_of(at, own_rows), own_rows)] = piece
    project(x_out, w_ref, q_ref, gate_ref, own_ref, score_scale)


def gather_heads(gated_refs, spot, wide):
    dim = gated_refs[0].shape[1]
    for step, ref in enumerate(gated_refs):
        at = pl.multiple_of((spot ^ step) * dim, dim)
        wide[:, pl.ds(at, dim)] = ref[...]


def term_kernel(spot_bits, layer_index, first_step, *refs):
    _, spot, _ = position(spot_bits)
    count = len(refs) - 2 - (1 if first_step else 0)
    gated_refs, (weight_ref, *before_refs, o_ref) = refs[:count], refs[count:]
    gated = jnp.concatenate([ref[...] for ref in gated_refs], axis=1)
    width = o_ref.shape[1]
    tile = min(width, 256)
    for first in range(0, width, tile):
        columns = slice(first, first + tile)
        weight = jnp.concatenate(
            [weight_ref[layer_index, spot ^ (first_step + at), :, columns] for at in range(count)],
            axis=0,
        )
        term = jnp.dot(gated, weight, preferred_element_type=jnp.float32)
        if before_refs:
            term = term + before_refs[0][:, columns]
        o_ref[:, columns] = term.astype(o_ref.dtype)


def step_kernel(spots, cores, spot_bits, score_scale, *refs):
    _, spot, core = position(spot_bits)
    term_refs, (x_ref, w_ref, x_own, q_ref, gate_ref, own_ref, x_next) = refs[:cores], refs[cores:]
    total = x_ref[...].astype(jnp.float32)
    for ref in term_refs:
        total = total + ref[...].astype(jnp.float32)
    x_next[...] = total.astype(jnp.bfloat16)
    own_rows = x_own.shape[0]
    at = (spot * cores + core) * own_rows
    x_own[...] = x_next[pl.ds(pl.multiple_of(at, own_rows), own_rows)]
    project(x_next, w_ref, q_ref, gate_ref, own_ref, score_scale)


def last_term_kernel(spots, cores, spot_bits, layer_index, *refs):
    _, spot, core = position(spot_bits)
    gated_refs, (weight_ref, *o_refs, wide, total) = refs[:spots], refs[spots:]
    gather_heads(gated_refs, spot, wide)
    own_rows, width = o_refs[0].shape
    weight = weight_ref[layer_index].reshape(wide.shape[1], width)
    total[...] = jnp.dot(wide[...], weight, preferred_element_type=jnp.float32)
    for shift, o_ref in enumerate(o_refs):
        at = lax.rem(core + shift, cores) * own_rows
        o_ref[...] = total[pl.ds(pl.multiple_of(at, own_rows), own_rows)].astype(jnp.bfloat16)


def add_kernel(*refs):
    total = refs[0][...].astype(jnp.float32)
    for ref in refs[1:-1]:
        total = total + ref[...].astype(jnp.float32)
    refs[-1][...] = total.astype(jnp.bfloat16)


def visit_history(spot_bits, masks, held, layer_index, scalar_refs, history_refs, q_wide, total):
    user_ref, offset_ref, length_ref = scalar_refs
    spot_masks, member_masks, spot_of_chip, row_count = masks
    spots = len(spot_masks)
    dim = total.shape[1]
    scale = 0.5 / math.sqrt(dim)
    chip, _, _ = position(spot_bits)
    spot_part = chip & spot_of_chip
    member_part = chip - spot_part

    def visit(ref, first, count, member, at):
        keys, values = [], []
        for piece in range(count):
            for block in range(ref.shape[2] // BLOCK):
                source = (member | (spot_part ^ spot_masks[at + piece])) * (ref.shape[2] // BLOCK) + block
                owner = user_ref[source]
                limit = length_ref[owner] - offset_ref[source] * BLOCK
                lanes = lax.broadcasted_iota(jnp.int32, (BLOCK, LANES), 1)
                sublanes = lax.broadcasted_iota(jnp.int32, (BLOCK, LANES), 0)
                seen = (lanes == owner) & (sublanes < limit)
                side = jnp.where(seen, 0.0, FAR).astype(jnp.bfloat16)
                at_rows = pl.ds(block * BLOCK, BLOCK)
                keys.append(jnp.concatenate([ref[first + piece, 0, at_rows], side], axis=1))
                values.append(ref[first + piece, 1, at_rows])
        half = lax.dot_general(
            q_wide[...],
            jnp.concatenate(keys, axis=0),
            (((1,), (1,)), ((), ())),
            preferred_element_type=jnp.float32,
        )
        weights = half_silu(half * scale).astype(jnp.bfloat16)
        total[...] += jnp.dot(
            weights, jnp.concatenate(values, axis=0), preferred_element_type=jnp.float32
        )

    if len(history_refs) == len(held):
        for ref, (mask, at) in zip(history_refs, held):
            visit(ref, 0, ref.shape[0], member_part ^ mask, at)
    else:

        @pl.loop(0, len(member_masks))
        def _(turn):
            member = turn * 0
            for i in range((len(member_masks) - 1).bit_length()):
                member = member | (((turn >> i) & 1) * member_masks[1 << i])
            visit(history_refs[0], turn * spots, spots, member, 0)


def attend_kernel(spot_bits, masks, held, layer_index, *refs):
    user_ref, offset_ref, length_ref, count_ref, q_ref, own_ref = refs[:6]
    history_refs, (q_wide, total) = refs[6:-2], refs[-2:]
    spot_masks, member_masks, spot_of_chip, row_count = masks
    spots = len(spot_masks)
    rows = q_ref.shape[0] // spots
    dim = q_ref.shape[1]
    user_count = length_ref.shape[0]
    chip, _, _ = position(spot_bits)
    member_part = chip - (chip & spot_of_chip)
    lane = lax.broadcasted_iota(jnp.int32, (1, LANES), 1)
    starts = jnp.zeros((1, LANES), jnp.int32)
    ends = jnp.zeros((1, LANES), jnp.int32)
    running = jnp.int32(0)
    for user in range(user_count):
        starts = jnp.where(lane == user, running, starts)
        running = running + count_ref[user]
        ends = jnp.where(lane == user, running, ends)
    q_wide[:, :dim] = q_ref[...]
    for at in range(spots):
        first = (member_part | spot_masks[at]) * row_count
        index = first + lax.broadcasted_iota(jnp.int32, (rows, LANES), 0)
        mine = (index >= starts) & (index < ends)
        q_wide[at * rows : (at + 1) * rows, dim:] = jnp.where(mine, 1.0, 0.0).astype(
            jnp.bfloat16
        )
    total[...] = own_ref[...]
    visit_history(
        spot_bits,
        masks,
        held,
        layer_index,
        (user_ref, offset_ref, length_ref),
        history_refs,
        q_wide,
        total,
    )


def finish_kernel(spot_bits, masks, held, layer_index, last, *refs):
    scalar_refs, (q_wide, before_ref, gate_ref), refs = refs[:3], refs[3:6], refs[6:]
    spots = len(masks[0])
    outs = spots if last else 1
    history_refs, o_refs, total = refs[: -outs - 1], refs[-outs - 1 : -1], refs[-1]
    rows = before_ref.shape[0] // spots
    _, spot, _ = position(spot_bits)
    total[...] = before_ref[...]
    if history_refs:
        visit_history(
            spot_bits, masks, held, layer_index, scalar_refs, history_refs, q_wide, total
        )
    full = total[...]
    centred = full - jnp.mean(full, axis=-1, keepdims=True)
    variance = jnp.mean(centred * centred, axis=-1, keepdims=True)
    gated = centred * lax.rsqrt(variance + 1e-05) * gate_ref[...].astype(jnp.float32)
    if not last:
        o_refs[0][...] = gated.astype(jnp.bfloat16)
        return
    total[...] = gated
    for step in range(spots):
        at_rows = pl.ds(pl.multiple_of((spot ^ step) * rows, rows), rows)
        o_refs[step][...] = total[at_rows].astype(jnp.bfloat16)


def body(
    candidate_rows,
    weight_in,
    weight_out,
    history_cache,
    block_user,
    block_offset,
    history_length,
    candidate_count,
):
    own_rows, model_width = candidate_rows.shape
    layers, model_again, heads_here, packed = weight_in.shape
    head_dim = packed // 4
    local_rows = history_cache.shape[2]
    cores = lax.axis_size("cand")
    chips = lax.axis_size("users")
    spots = heads_here
    groups = chips // spots
    row_count = own_rows * cores
    all_rows = row_count * spots
    score_scale = 1.0 / math.sqrt(head_dim)

    bits = list(range(chips.bit_length() - 1))
    spot_bits = sorted((bits[::2] + bits[1::2])[: spots.bit_length() - 1])
    member_bits = [b for b in bits if b not in spot_bits]

    def mask_of(number, places):
        return sum(((number >> i) & 1) << b for i, b in enumerate(places))

    def swap(value, mask):
        return lax.ppermute(value, "users", [(u, u ^ mask) for u in range(chips)])

    def trade_spots(values, diagonal_first=True):
        steps = range(1, spots)
        moved = {0: values[0]}
        for m in reversed(steps) if diagonal_first else steps:
            moved[m] = swap(values[m], mask_of(m, spot_bits))
        return [moved[m] for m in range(spots)]

    def gather_spots(value):
        found = [value]
        for bit in reversed(range(len(spot_bits))):
            mask = 1 << spot_bits[bit]
            found = [(v, swap(v, mask)) for v in found]
            found = [v for v, _ in found] + [w for _, w in found]
        order = [0]
        for bit in reversed(range(len(spot_bits))):
            order = order + [o | (1 << bit) for o in order]
        return [found[order.index(m)] for m in range(spots)]

    def shift_core(value, step):
        pairs = [(c, (c + step) % cores) for c in range(cores)]
        return lax.ppermute(value, "cand", pairs)

    spot_masks = [mask_of(m, spot_bits) for m in range(spots)]
    member_masks = [mask_of(m, member_bits) for m in range(groups)]

    masks = (spot_masks, member_masks, spot_masks[-1], row_count)

    def gather_members(pieces):
        if groups <= 2:
            return [pieces] + [swap(pieces, mask) for mask in member_masks[1:]]
        chips_of = [[mask_of(s, spot_bits) | m for m in member_masks] for s in range(spots)]
        return [
            lax.all_gather(pieces, "users", axis=0, axis_index_groups=chips_of, tiled=True)
        ]

    def after(value, *others):
        return lax.optimization_barrier((value,) + others)[0]

    def kernel_call(kernel, outs, name, operands, scratch=(), limit=8, specs=None):
        results = pl.pallas_call(
            kernel,
            out_shape=[jax.ShapeDtypeStruct(*out) for out in outs],
            in_specs=specs or [VMEM_SPEC] * len(operands),
            out_specs=[VMEM_SPEC] * len(outs),
            scratch_shapes=scratch,
            compiler_params=pltpu.CompilerParams(vmem_limit_bytes=limit * MIB),
            name=name,
        )(*operands)
        return list(results)

    def pick_head(layer_index):
        rows = min(model_width, 128)
        chunks = model_width // rows
        return kernel_call(
            functools.partial(pick_head_kernel, layer_index, spot_bits),
            [((model_width, packed), weight_in.dtype)],
            "pick_head",
            [weight_in],
            [
                pltpu.VMEM((chunks, rows, heads_here, packed), weight_in.dtype),
                pltpu.SemaphoreType.DMA((chunks,)),
            ],
            51,
            [pl.BlockSpec(memory_space=pl.ANY)],
        )[0]

    def order_history():
        shape = (layers, 2, local_rows, head_dim)
        return kernel_call(
            functools.partial(order_history_kernel, spot_bits),
            [(shape, jnp.bfloat16)] * spots,
            "order_history",
            [history_cache],
            [pltpu.VMEM((spots,) + shape, jnp.bfloat16)],
            4,
        )

    def join_layers(pieces):
        shape = (spots, 2, local_rows, head_dim)
        first, *later = kernel_call(
            functools.partial(join_layers_kernel, spots),
            [(shape, jnp.bfloat16)] * layers,
            "join_layers",
            list(pieces),
        )
        return first, later

    def halves(pieces):
        shape = (pieces.shape[0] // 2,) + pieces.shape[1:]
        return kernel_call(halves_kernel, [(shape, pieces.dtype)] * 2, "halves", [pieces])

    def join(pieces):
        if len(pieces) == 1:
            return pieces[0][None]
        shape = (len(pieces),) + pieces[0].shape
        return kernel_call(join_kernel, [(shape, pieces[0].dtype)], "join", list(pieces))[0]

    def together(*values):
        return lax.optimization_barrier(values)

    pieces, first_weight = together(trade_spots(order_history()), pick_head(0))
    first, later = join_layers(pieces)
    x_pieces = trade_spots([after(candidate_rows, first)] * spots)
    crossed = groups == 4
    if crossed:
        near_mask, far_mask = member_masks[1:3]
        far = swap(first, far_mask)
        near = swap(first, near_mask)
        far, near = together(far, near)
        onward = swap(far, near_mask)
        x_pieces[1:] = [after(piece, far) for piece in x_pieces[1:]]
        history = [[first, near, far, onward]]
    else:
        history = [gather_members(first)]
    x_group = x_pieces + [shift_core(piece, s) for s in range(1, cores) for piece in x_pieces]

    scalars = [block_user, block_offset, history_length, candidate_count]
    one_head = (all_rows, head_dim)
    head_outs = [(one_head, jnp.bfloat16), (one_head, jnp.bfloat16), (one_head, jnp.float32)]
    x, *projected = kernel_call(
        functools.partial(begin_kernel, spots, cores, spot_bits, score_scale),
        [((all_rows, model_width), jnp.bfloat16)] + head_outs,
        "begin",
        x_group + [first_weight],
    )

    for layer_index in range(layers):
        last = layer_index + 1 == layers
        outs = [((row_count, head_dim), jnp.bfloat16)] * spots if last else head_outs[:1]
        query, gate, own = projected
        held, split = (), 1
        if crossed:
            parts = 2 if layer_index else 1
            cuts = [spots // parts * part for part in range(parts)]
            held = ((0, 0), (near_mask, 0))
            held += tuple((m, at) for m in (far_mask, near_mask | far_mask) for at in cuts)
            split = 2 + parts + parts // 2
        ready, coming = history[layer_index][:split], history[layer_index][split:]
        operands = scalars + [query, own] + ready
        wide_query, total = kernel_call(
            functools.partial(attend_kernel, spot_bits, masks, held[:split], layer_index),
            [((all_rows, head_dim + LANES), jnp.bfloat16), (one_head, jnp.float32)],
            "attend",
            operands,
            (),
            16,
            [SMEM_SPEC] * 4 + [VMEM_SPEC] * (len(operands) - 4),
        )
        operands = scalars[:3] + [wide_query, total, gate] + coming
        gated = kernel_call(
            functools.partial(finish_kernel, spot_bits, masks, held[split:], layer_index, last),
            outs,
            "finish",
            operands,
            [pltpu.VMEM(one_head, jnp.float32)],
            16,
            [SMEM_SPEC] * 3 + [VMEM_SPEC] * (len(operands) - 3),
        )
        if not last:
            gated = trade_spots(list(gated) * spots, False)
            next_weight = pick_head(layer_index + 1)
            if crossed:
                whole = after(later[layer_index], far, near)
                far, near = swap(whole, far_mask), swap(whole, near_mask)
                far = halves(after(far, near, gated[1]))
                ahead = swap(far[0], near_mask)
                early, far, next_weight = together(gated[:-1], far, next_weight)
                late, ahead = together(gated[-1:], ahead)
                parts = [(0, early), (spots - 1, late)]
                arrays = [whole, near] + far + [ahead, swap(far[1], near_mask)]
            else:
                arrays = gather_members(later[layer_index])
                parts = [(0, gated)]
            terms = []
            for first_step, heads in parts:
                terms = kernel_call(
                    functools.partial(term_kernel, spot_bits, layer_index, first_step),
                    [
                        (
                            (all_rows, model_width),
                            jnp.bfloat16 if first_step + len(heads) == spots else jnp.float32,
                        )
                    ],
                    "term",
                    heads + [weight_out] + terms,
                )
            terms = terms + [shift_core(terms[0], s) for s in range(1, cores)]
            history.append(arrays)
            x, *projected = kernel_call(
                functools.partial(step_kernel, spots, cores, spot_bits, score_scale),
                [((own_rows, model_width), jnp.bfloat16)] + head_outs,
                "step",
                terms + [x, next_weight],
                [pltpu.VMEM((all_rows, model_width), jnp.bfloat16)],
                12,
            )
        else:
            terms = kernel_call(
                functools.partial(last_term_kernel, spots, cores, spot_bits, layer_index),
                [((own_rows, model_width), jnp.bfloat16)] * cores,
                "last_term",
                trade_spots(gated) + [weight_out],
                [
                    pltpu.VMEM((row_count, spots * head_dim), jnp.bfloat16),
                    pltpu.VMEM((row_count, model_width), jnp.float32),
                ],
            )
            terms = terms[:1] + [shift_core(terms[s], s) for s in range(1, cores)]
            (out,) = kernel_call(
                add_kernel, [((own_rows, model_width), jnp.bfloat16)], "add", [x] + terms
            )
    return out


def solution(mesh):
    placed = (
        P(("users", "cand"), None),
        P(None, None, "cand", None),
        P(None, "cand", None, None),
        P(None, None, "users", "cand", None),
        P(),
        P(),
        P(),
        P(),
    )
    return jax.shard_map(
        body, mesh=mesh, in_specs=placed, out_specs=P(("users", "cand"), None), check_vma=False
    )
```

```python
import functools
import math

import jax
import jax.numpy as jnp
from jax import lax
from jax.experimental import pallas as pl
from jax.experimental.pallas import tpu as pltpu
from jax.sharding import PartitionSpec as P

BLOCK = 128
LANES = 128
FAR = -1e30
MIB = 1024 * 1024

VMEM_SPEC = pl.BlockSpec(memory_space=pltpu.VMEM)
SMEM_SPEC = pl.BlockSpec(memory_space=pltpu.SMEM)


def half_silu(half):
    return half + half * jnp.tanh(half)


def position(spot_bits):
    chip = lax.axis_index("users")
    spot = sum((((chip >> b) & 1) << i for i, b in enumerate(spot_bits)), chip * 0)
    return chip, spot, lax.axis_index("cand")


def order_history_kernel(spot_bits, h_ref, *refs):
    o_refs, pieces = refs[:-1], refs[-1]
    _, spot, _ = position(spot_bits)
    for layer_index in range(h_ref.shape[0]):
        for kind in range(h_ref.shape[1]):
            by_head = jnp.swapaxes(h_ref[layer_index, kind], 0, 1)
            for head in range(h_ref.shape[3]):
                pieces[spot ^ head, layer_index, kind] = by_head[head]
    for step, o_ref in enumerate(o_refs):
        o_ref[...] = pieces[step]


def join_layers_kernel(count, *refs):
    for layer_index, o_ref in enumerate(refs[count:]):
        for at, ref in enumerate(refs[:count]):
            o_ref[at] = ref[layer_index]


def halves_kernel(i_ref, low_ref, high_ref):
    size = low_ref.shape[0]
    low_ref[...] = i_ref[:size]
    high_ref[...] = i_ref[size:]


def join_kernel(*refs):
    o_ref = refs[-1]
    for at, ref in enumerate(refs[:-1]):
        o_ref[at] = ref[...]


def pick_head_kernel(layer_index, spot_bits, w_ref, o_ref, held, sems):
    _, spot, _ = position(spot_bits)
    chunks, rows = held.shape[:2]
    copies = [
        pltpu.make_async_copy(
            w_ref.at[layer_index, pl.ds(at * rows, rows)], held.at[at], sems.at[at]
        )
        for at in range(chunks)
    ]
    for copy in copies:
        copy.start()
    for at, copy in enumerate(copies):
        copy.wait()
        by_head = jnp.swapaxes(held[at], 0, 1)
        for head in range(held.shape[2]):

            @pl.when(spot == head)
            def _(at=at, head=head, by_head=by_head):
                o_ref[at * rows : (at + 1) * rows] = by_head[head]


def project(x_ref, w_ref, q_ref, gate_ref, own_ref, score_scale):
    dim = q_ref.shape[1]

    def part(first):
        w = w_ref[:, first * dim : (first + 2) * dim]
        mixed = jnp.dot(x_ref[...], w, preferred_element_type=jnp.float32)
        return half_silu(mixed * 0.5).astype(jnp.bfloat16)

    tail = part(2)
    query = tail[:, :dim]
    q_ref[...] = query
    score = jnp.sum(
        query.astype(jnp.float32) * tail[:, dim:].astype(jnp.float32), axis=-1, keepdims=True
    )
    weight = half_silu(score * (0.5 * score_scale)).astype(jnp.bfloat16).astype(jnp.float32)
    front = part(0)
    gate_ref[...] = front[:, :dim]
    own_ref[...] = weight * front[:, dim:].astype(jnp.float32)


def begin_kernel(spots, cores, spot_bits, score_scale, *refs):
    _, spot, core_here = position(spot_bits)
    x_refs, (w_ref, x_out, q_ref, gate_ref, own_ref) = refs[:-5], refs[-5:]
    own_rows = x_out.shape[0] // (spots * cores)
    for shift in range(cores):
        core = lax.rem(core_here + (cores - shift), cores)
        for step in range(spots):
            piece = x_refs[shift * spots + step][...]
            at = ((spot ^ step) * cores + core) * own_rows
            x_out[pl.ds(pl.multiple_of(at, own_rows), own_rows)] = piece
    project(x_out, w_ref, q_ref, gate_ref, own_ref, score_scale)


def gather_heads(gated_refs, spot, wide):
    dim = gated_refs[0].shape[1]
    for step, ref in enumerate(gated_refs):
        at = pl.multiple_of((spot ^ step) * dim, dim)
        wide[:, pl.ds(at, dim)] = ref[...]


def term_kernel(spot_bits, layer_index, first_step, *refs):
    _, spot, _ = position(spot_bits)
    count = len(refs) - 2 - (1 if first_step else 0)
    gated_refs, (weight_ref, *before_refs, o_ref) = refs[:count], refs[count:]
    gated = jnp.concatenate([ref[...] for ref in gated_refs], axis=1)
    width = o_ref.shape[1]
    tile = min(width, 256)
    for first in range(0, width, tile):
        columns = slice(first, first + tile)
        weight = jnp.concatenate(
            [weight_ref[layer_index, spot ^ (first_step + at), :, columns] for at in range(count)],
            axis=0,
        )
        term = jnp.dot(gated, weight, preferred_element_type=jnp.float32)
        if before_refs:
            term = term + before_refs[0][:, columns]
        o_ref[:, columns] = term.astype(o_ref.dtype)


def step_kernel(spots, cores, spot_bits, score_scale, *refs):
    _, spot, core = position(spot_bits)
    term_refs, (x_ref, w_ref, x_own, q_ref, gate_ref, own_ref, x_next) = refs[:cores], refs[cores:]
    total = x_ref[...].astype(jnp.float32)
    for ref in term_refs:
        total = total + ref[...].astype(jnp.float32)
    x_next[...] = total.astype(jnp.bfloat16)
    own_rows = x_own.shape[0]
    at = (spot * cores + core) * own_rows
    x_own[...] = x_next[pl.ds(pl.multiple_of(at, own_rows), own_rows)]
    project(x_next, w_ref, q_ref, gate_ref, own_ref, score_scale)


def last_term_kernel(spots, cores, spot_bits, layer_index, *refs):
    _, spot, core = position(spot_bits)
    gated_refs, (weight_ref, *o_refs, wide, total) = refs[:spots], refs[spots:]
    gather_heads(gated_refs, spot, wide)
    own_rows, width = o_refs[0].shape
    weight = weight_ref[layer_index].reshape(wide.shape[1], width)
    total[...] = jnp.dot(wide[...], weight, preferred_element_type=jnp.float32)
    for shift, o_ref in enumerate(o_refs):
        at = lax.rem(core + shift, cores) * own_rows
        o_ref[...] = total[pl.ds(pl.multiple_of(at, own_rows), own_rows)].astype(jnp.bfloat16)


def add_kernel(*refs):
    total = refs[0][...].astype(jnp.float32)
    for ref in refs[1:-1]:
        total = total + ref[...].astype(jnp.float32)
    refs[-1][...] = total.astype(jnp.bfloat16)


def visit_history(spot_bits, masks, held, layer_index, scalar_refs, history_refs, q_wide, total):
    user_ref, offset_ref, length_ref = scalar_refs
    spot_masks, member_masks, spot_of_chip, row_count = masks
    spots = len(spot_masks)
    dim = total.shape[1]
    scale = 0.5 / math.sqrt(dim)
    chip, _, _ = position(spot_bits)
    spot_part = chip & spot_of_chip
    member_part = chip - spot_part

    def visit(ref, first, count, member, at):
        keys, values = [], []
        for piece in range(count):
            for block in range(ref.shape[2] // BLOCK):
                source = (member | (spot_part ^ spot_masks[at + piece])) * (ref.shape[2] // BLOCK) + block
                owner = user_ref[source]
                limit = length_ref[owner] - offset_ref[source] * BLOCK
                lanes = lax.broadcasted_iota(jnp.int32, (BLOCK, LANES), 1)
                sublanes = lax.broadcasted_iota(jnp.int32, (BLOCK, LANES), 0)
                seen = (lanes == owner) & (sublanes < limit)
                side = jnp.where(seen, 0.0, FAR).astype(jnp.bfloat16)
                at_rows = pl.ds(block * BLOCK, BLOCK)
                keys.append(jnp.concatenate([ref[first + piece, 0, at_rows], side], axis=1))
                values.append(ref[first + piece, 1, at_rows])
        half = lax.dot_general(
            q_wide[...],
            jnp.concatenate(keys, axis=0),
            (((1,), (1,)), ((), ())),
            preferred_element_type=jnp.float32,
        )
        weights = half_silu(half * scale).astype(jnp.bfloat16)
        total[...] += jnp.dot(
            weights, jnp.concatenate(values, axis=0), preferred_element_type=jnp.float32
        )

    if len(history_refs) == len(held):
        for ref, (mask, at) in zip(history_refs, held):
            visit(ref, 0, ref.shape[0], member_part ^ mask, at)
    else:

        @pl.loop(0, len(member_masks))
        def _(turn):
            member = turn * 0
            for i in range((len(member_masks) - 1).bit_length()):
                member = member | (((turn >> i) & 1) * member_masks[1 << i])
            visit(history_refs[0], turn * spots, spots, member, 0)


def attend_kernel(spot_bits, masks, held, layer_index, *refs):
    user_ref, offset_ref, length_ref, count_ref, q_ref, own_ref = refs[:6]
    history_refs, (q_wide, total) = refs[6:-2], refs[-2:]
    spot_masks, member_masks, spot_of_chip, row_count = masks
    spots = len(spot_masks)
    rows = q_ref.shape[0] // spots
    dim = q_ref.shape[1]
    user_count = length_ref.shape[0]
    chip, _, _ = position(spot_bits)
    member_part = chip - (chip & spot_of_chip)
    lane = lax.broadcasted_iota(jnp.int32, (1, LANES), 1)
    starts = jnp.zeros((1, LANES), jnp.int32)
    ends = jnp.zeros((1, LANES), jnp.int32)
    running = jnp.int32(0)
    for user in range(user_count):
        starts = jnp.where(lane == user, running, starts)
        running = running + count_ref[user]
        ends = jnp.where(lane == user, running, ends)
    q_wide[:, :dim] = q_ref[...]
    for at in range(spots):
        first = (member_part | spot_masks[at]) * row_count
        index = first + lax.broadcasted_iota(jnp.int32, (rows, LANES), 0)
        mine = (index >= starts) & (index < ends)
        q_wide[at * rows : (at + 1) * rows, dim:] = jnp.where(mine, 1.0, 0.0).astype(
            jnp.bfloat16
        )
    total[...] = own_ref[...]
    visit_history(
        spot_bits,
        masks,
        held,
        layer_index,
        (user_ref, offset_ref, length_ref),
        history_refs,
        q_wide,
        total,
    )


def finish_kernel(spot_bits, masks, held, layer_index, last, *refs):
    scalar_refs, (q_wide, before_ref, gate_ref), refs = refs[:3], refs[3:6], refs[6:]
    spots = len(masks[0])
    outs = spots if last else 1
    history_refs, o_refs, total = refs[: -outs - 1], refs[-outs - 1 : -1], refs[-1]
    rows = before_ref.shape[0] // spots
    _, spot, _ = position(spot_bits)
    total[...] = before_ref[...]
    if history_refs:
        visit_history(
            spot_bits, masks, held, layer_index, scalar_refs, history_refs, q_wide, total
        )
    full = total[...]
    centred = full - jnp.mean(full, axis=-1, keepdims=True)
    variance = jnp.mean(centred * centred, axis=-1, keepdims=True)
    gated = centred * lax.rsqrt(variance + 1e-05) * gate_ref[...].astype(jnp.float32)
    if not last:
        o_refs[0][...] = gated.astype(jnp.bfloat16)
        return
    total[...] = gated
    for step in range(spots):
        at_rows = pl.ds(pl.multiple_of((spot ^ step) * rows, rows), rows)
        o_refs[step][...] = total[at_rows].astype(jnp.bfloat16)


def body(
    candidate_rows,
    weight_in,
    weight_out,
    history_cache,
    block_user,
    block_offset,
    history_length,
    candidate_count,
):
    own_rows, model_width = candidate_rows.shape
    layers, model_again, heads_here, packed = weight_in.shape
    head_dim = packed // 4
    local_rows = history_cache.shape[2]
    cores = lax.axis_size("cand")
    chips = lax.axis_size("users")
    spots = heads_here
    groups = chips // spots
    row_count = own_rows * cores
    all_rows = row_count * spots
    score_scale = 1.0 / math.sqrt(head_dim)

    bits = list(range(chips.bit_length() - 1))
    spot_bits = sorted((bits[::2] + bits[1::2])[: spots.bit_length() - 1])
    member_bits = [b for b in bits if b not in spot_bits]

    def mask_of(number, places):
        return sum(((number >> i) & 1) << b for i, b in enumerate(places))

    def swap(value, mask):
        return lax.ppermute(value, "users", [(u, u ^ mask) for u in range(chips)])

    def trade_spots(values, diagonal_first=True):
        steps = range(1, spots)
        moved = {0: values[0]}
        for m in reversed(steps) if diagonal_first else steps:
            moved[m] = swap(values[m], mask_of(m, spot_bits))
        return [moved[m] for m in range(spots)]

    def gather_spots(value):
        found = [value]
        for bit in reversed(range(len(spot_bits))):
            mask = 1 << spot_bits[bit]
            found = [(v, swap(v, mask)) for v in found]
            found = [v for v, _ in found] + [w for _, w in found]
        order = [0]
        for bit in reversed(range(len(spot_bits))):
            order = order + [o | (1 << bit) for o in order]
        return [found[order.index(m)] for m in range(spots)]

    def shift_core(value, step):
        pairs = [(c, (c + step) % cores) for c in range(cores)]
        return lax.ppermute(value, "cand", pairs)

    spot_masks = [mask_of(m, spot_bits) for m in range(spots)]
    member_masks = [mask_of(m, member_bits) for m in range(groups)]

    masks = (spot_masks, member_masks, spot_masks[-1], row_count)

    def gather_members(pieces):
        if groups <= 2:
            return [pieces] + [swap(pieces, mask) for mask in member_masks[1:]]
        chips_of = [[mask_of(s, spot_bits) | m for m in member_masks] for s in range(spots)]
        return [
            lax.all_gather(pieces, "users", axis=0, axis_index_groups=chips_of, tiled=True)
        ]

    def after(value, *others):
        return lax.optimization_barrier((value,) + others)[0]

    def kernel_call(kernel, outs, name, operands, scratch=(), limit=8, specs=None):
        results = pl.pallas_call(
            kernel,
            out_shape=[jax.ShapeDtypeStruct(*out) for out in outs],
            in_specs=specs or [VMEM_SPEC] * len(operands),
            out_specs=[VMEM_SPEC] * len(outs),
            scratch_shapes=scratch,
            compiler_params=pltpu.CompilerParams(vmem_limit_bytes=limit * MIB),
            name=name,
        )(*operands)
        return list(results)

    def pick_head(layer_index):
        rows = min(model_width, 128)
        chunks = model_width // rows
        return kernel_call(
            functools.partial(pick_head_kernel, layer_index, spot_bits),
            [((model_width, packed), weight_in.dtype)],
            "pick_head",
            [weight_in],
            [
                pltpu.VMEM((chunks, rows, heads_here, packed), weight_in.dtype),
                pltpu.SemaphoreType.DMA((chunks,)),
            ],
            51,
            [pl.BlockSpec(memory_space=pl.ANY)],
        )[0]

    def order_history():
        shape = (layers, 2, local_rows, head_dim)
        return kernel_call(
            functools.partial(order_history_kernel, spot_bits),
            [(shape, jnp.bfloat16)] * spots,
            "order_history",
            [history_cache],
            [pltpu.VMEM((spots,) + shape, jnp.bfloat16)],
            4,
        )

    def join_layers(pieces):
        shape = (spots, 2, local_rows, head_dim)
        first, *later = kernel_call(
            functools.partial(join_layers_kernel, spots),
            [(shape, jnp.bfloat16)] * layers,
            "join_layers",
            list(pieces),
        )
        return first, later

    def halves(pieces):
        shape = (pieces.shape[0] // 2,) + pieces.shape[1:]
        return kernel_call(halves_kernel, [(shape, pieces.dtype)] * 2, "halves", [pieces])

    def join(pieces):
        if len(pieces) == 1:
            return pieces[0][None]
        shape = (len(pieces),) + pieces[0].shape
        return kernel_call(join_kernel, [(shape, pieces[0].dtype)], "join", list(pieces))[0]

    def together(*values):
        return lax.optimization_barrier(values)

    sibling_rows = [shift_core(candidate_rows, s) for s in range(1, cores)]
    pieces, first_weight, sibling_rows = together(
        trade_spots(order_history()), pick_head(0), sibling_rows
    )
    first, later = join_layers(pieces)
    x_pieces = trade_spots([after(candidate_rows, first)] * spots)
    crossed = groups == 4
    if crossed:
        near_mask, far_mask = member_masks[1:3]
        far = swap(first, far_mask)
        near = swap(first, near_mask)
        far, near = together(far, near)
        onward = swap(far, near_mask)
        x_pieces[1:] = [after(piece, far) for piece in x_pieces[1:]]
        history = [[first, near, far, onward]]
    else:
        history = [gather_members(first)]
    x_group = list(x_pieces)
    for s in range(1, cores):
        x_group += [sibling_rows[s - 1]] + [shift_core(piece, s) for piece in x_pieces[1:]]

    scalars = [block_user, block_offset, history_length, candidate_count]
    one_head = (all_rows, head_dim)
    head_outs = [(one_head, jnp.bfloat16), (one_head, jnp.bfloat16), (one_head, jnp.float32)]
    x, *projected = kernel_call(
        functools.partial(begin_kernel, spots, cores, spot_bits, score_scale),
        [((all_rows, model_width), jnp.bfloat16)] + head_outs,
        "begin",
        x_group + [first_weight],
    )

    for layer_index in range(layers):
        last = layer_index + 1 == layers
        outs = [((row_count, head_dim), jnp.bfloat16)] * spots if last else head_outs[:1]
        query, gate, own = projected
        held, split = (), 1
        if crossed:
            parts = 2 if layer_index else 1
            cuts = [spots // parts * part for part in range(parts)]
            held = ((0, 0), (near_mask, 0))
            held += tuple((m, at) for m in (far_mask, near_mask | far_mask) for at in cuts)
            split = 2 + parts + parts // 2
        ready, coming = history[layer_index][:split], history[layer_index][split:]
        operands = scalars + [query, own] + ready
        wide_query, total = kernel_call(
            functools.partial(attend_kernel, spot_bits, masks, held[:split], layer_index),
            [((all_rows, head_dim + LANES), jnp.bfloat16), (one_head, jnp.float32)],
            "attend",
            operands,
            (),
            16,
            [SMEM_SPEC] * 4 + [VMEM_SPEC] * (len(operands) - 4),
        )
        operands = scalars[:3] + [wide_query, total, gate] + coming
        gated = kernel_call(
            functools.partial(finish_kernel, spot_bits, masks, held[split:], layer_index, last),
            outs,
            "finish",
            operands,
            [pltpu.VMEM(one_head, jnp.float32)],
            16,
            [SMEM_SPEC] * 3 + [VMEM_SPEC] * (len(operands) - 3),
        )
        if not last:
            gated = trade_spots(list(gated) * spots, False)
            next_weight = pick_head(layer_index + 1)
            if crossed:
                whole = after(later[layer_index], far, near)
                far, near = swap(whole, far_mask), swap(whole, near_mask)
                far = halves(after(far, near, gated[1]))
                ahead = swap(far[0], near_mask)
                early, far, next_weight = together(gated[:-1], far, next_weight)
                late, ahead = together(gated[-1:], ahead)
                parts = [(0, early), (spots - 1, late)]
                arrays = [whole, near] + far + [ahead, swap(far[1], near_mask)]
            else:
                arrays = gather_members(later[layer_index])
                parts = [(0, gated)]
            terms = []
            for first_step, heads in parts:
                terms = kernel_call(
                    functools.partial(term_kernel, spot_bits, layer_index, first_step),
                    [
                        (
                            (all_rows, model_width),
                            jnp.bfloat16 if first_step + len(heads) == spots else jnp.float32,
                        )
                    ],
                    "term",
                    heads + [weight_out] + terms,
                )
            terms = terms + [shift_core(terms[0], s) for s in range(1, cores)]
            history.append(arrays)
            x, *projected = kernel_call(
                functools.partial(step_kernel, spots, cores, spot_bits, score_scale),
                [((own_rows, model_width), jnp.bfloat16)] + head_outs,
                "step",
                terms + [x, next_weight],
                [pltpu.VMEM((all_rows, model_width), jnp.bfloat16)],
                12,
            )
        else:
            terms = kernel_call(
                functools.partial(last_term_kernel, spots, cores, spot_bits, layer_index),
                [((own_rows, model_width), jnp.bfloat16)] * cores,
                "last_term",
                trade_spots(gated) + [weight_out],
                [
                    pltpu.VMEM((row_count, spots * head_dim), jnp.bfloat16),
                    pltpu.VMEM((row_count, model_width), jnp.float32),
                ],
            )
            terms = terms[:1] + [shift_core(terms[s], s) for s in range(1, cores)]
            (out,) = kernel_call(
                add_kernel, [((own_rows, model_width), jnp.bfloat16)], "add", [x] + terms
            )
    return out


def solution(mesh):
    placed = (
        P(("users", "cand"), None),
        P(None, None, "cand", None),
        P(None, "cand", None, None),
        P(None, None, "users", "cand", None),
        P(),
        P(),
        P(),
        P(),
    )
    return jax.shard_map(
        body, mesh=mesh, in_specs=placed, out_specs=P(("users", "cand"), None), check_vma=False
    )
```

```python
import functools
import math

import jax
import jax.numpy as jnp
from jax import lax
from jax.experimental import pallas as pl
from jax.experimental.pallas import tpu as pltpu
from jax.sharding import PartitionSpec as P

BLOCK = 128
LANES = 128
FAR = -1e30
MIB = 1024 * 1024

VMEM_SPEC = pl.BlockSpec(memory_space=pltpu.VMEM)
SMEM_SPEC = pl.BlockSpec(memory_space=pltpu.SMEM)


def half_silu(half):
    return half + half * jnp.tanh(half)


def position(spot_bits):
    chip = lax.axis_index("users")
    spot = sum((((chip >> b) & 1) << i for i, b in enumerate(spot_bits)), chip * 0)
    return chip, spot, lax.axis_index("cand")


def order_history_kernel(spot_bits, h_ref, *refs):
    o_refs, pieces = refs[:-1], refs[-1]
    _, spot, _ = position(spot_bits)
    for layer_index in range(h_ref.shape[0]):
        for kind in range(h_ref.shape[1]):
            by_head = jnp.swapaxes(h_ref[layer_index, kind], 0, 1)
            for head in range(h_ref.shape[3]):
                pieces[spot ^ head, layer_index, kind] = by_head[head]
    for step, o_ref in enumerate(o_refs):
        o_ref[...] = pieces[step]


def join_layers_kernel(count, *refs):
    for layer_index, o_ref in enumerate(refs[count:]):
        for at, ref in enumerate(refs[:count]):
            o_ref[at] = ref[layer_index]


def halves_kernel(i_ref, low_ref, high_ref):
    size = low_ref.shape[0]
    low_ref[...] = i_ref[:size]
    high_ref[...] = i_ref[size:]


def join_kernel(*refs):
    o_ref = refs[-1]
    for at, ref in enumerate(refs[:-1]):
        o_ref[at] = ref[...]


def pick_head_kernel(layer_index, spot_bits, w_ref, o_ref, held, sems):
    _, spot, _ = position(spot_bits)
    chunks, rows = held.shape[:2]
    copies = [
        pltpu.make_async_copy(
            w_ref.at[layer_index, pl.ds(at * rows, rows)], held.at[at], sems.at[at]
        )
        for at in range(chunks)
    ]
    for copy in copies:
        copy.start()
    for at, copy in enumerate(copies):
        copy.wait()
        by_head = jnp.swapaxes(held[at], 0, 1)
        for head in range(held.shape[2]):

            @pl.when(spot == head)
            def _(at=at, head=head, by_head=by_head):
                o_ref[at * rows : (at + 1) * rows] = by_head[head]


def project(x_ref, w_ref, q_ref, gate_ref, own_ref, score_scale):
    dim = q_ref.shape[1]

    def part(first):
        w = w_ref[:, first * dim : (first + 2) * dim]
        mixed = jnp.dot(x_ref[...], w, preferred_element_type=jnp.float32)
        return half_silu(mixed * 0.5).astype(jnp.bfloat16)

    tail = part(2)
    query = tail[:, :dim]
    q_ref[...] = query
    score = jnp.sum(
        query.astype(jnp.float32) * tail[:, dim:].astype(jnp.float32), axis=-1, keepdims=True
    )
    weight = half_silu(score * (0.5 * score_scale)).astype(jnp.bfloat16).astype(jnp.float32)
    front = part(0)
    gate_ref[...] = front[:, :dim]
    own_ref[...] = weight * front[:, dim:].astype(jnp.float32)


def begin_kernel(spots, cores, spot_bits, score_scale, *refs):
    _, spot, core_here = position(spot_bits)
    x_refs, (w_ref, x_out, q_ref, gate_ref, own_ref) = refs[:-5], refs[-5:]
    own_rows = x_out.shape[0] // (spots * cores)
    for shift in range(cores):
        core = lax.rem(core_here + (cores - shift), cores)
        for step in range(spots):
            piece = x_refs[shift * spots + step][...]
            at = ((spot ^ step) * cores + core) * own_rows
            x_out[pl.ds(pl.multiple_of(at, own_rows), own_rows)] = piece
    project(x_out, w_ref, q_ref, gate_ref, own_ref, score_scale)


def gather_heads(gated_refs, spot, wide):
    dim = gated_refs[0].shape[1]
    for step, ref in enumerate(gated_refs):
        at = pl.multiple_of((spot ^ step) * dim, dim)
        wide[:, pl.ds(at, dim)] = ref[...]


def term_kernel(spot_bits, layer_index, first_step, *refs):
    _, spot, _ = position(spot_bits)
    count = len(refs) - 2 - (1 if first_step else 0)
    gated_refs, (weight_ref, *before_refs, o_ref) = refs[:count], refs[count:]
    gated = jnp.concatenate([ref[...] for ref in gated_refs], axis=1)
    width = o_ref.shape[1]
    tile = min(width, 256)
    for first in range(0, width, tile):
        columns = slice(first, first + tile)
        weight = jnp.concatenate(
            [weight_ref[layer_index, spot ^ (first_step + at), :, columns] for at in range(count)],
            axis=0,
        )
        term = jnp.dot(gated, weight, preferred_element_type=jnp.float32)
        if before_refs:
            term = term + before_refs[0][:, columns]
        o_ref[:, columns] = term.astype(o_ref.dtype)


def step_kernel(spots, cores, spot_bits, score_scale, *refs):
    _, spot, core = position(spot_bits)
    term_refs, (x_ref, w_ref, x_own, q_ref, gate_ref, own_ref, x_next) = refs[:cores], refs[cores:]
    total = x_ref[...].astype(jnp.float32)
    for ref in term_refs:
        total = total + ref[...].astype(jnp.float32)
    x_next[...] = total.astype(jnp.bfloat16)
    own_rows = x_own.shape[0]
    at = (spot * cores + core) * own_rows
    x_own[...] = x_next[pl.ds(pl.multiple_of(at, own_rows), own_rows)]
    project(x_next, w_ref, q_ref, gate_ref, own_ref, score_scale)


def last_term_kernel(spots, cores, spot_bits, layer_index, *refs):
    _, spot, core = position(spot_bits)
    gated_refs, (weight_ref, *o_refs, wide, total) = refs[:spots], refs[spots:]
    gather_heads(gated_refs, spot, wide)
    own_rows, width = o_refs[0].shape
    weight = weight_ref[layer_index].reshape(wide.shape[1], width)
    total[...] = jnp.dot(wide[...], weight, preferred_element_type=jnp.float32)
    for shift, o_ref in enumerate(o_refs):
        at = lax.rem(core + shift, cores) * own_rows
        o_ref[...] = total[pl.ds(pl.multiple_of(at, own_rows), own_rows)].astype(jnp.bfloat16)


def add_kernel(*refs):
    total = refs[0][...].astype(jnp.float32)
    for ref in refs[1:-1]:
        total = total + ref[...].astype(jnp.float32)
    refs[-1][...] = total.astype(jnp.bfloat16)


def visit_history(spot_bits, masks, held, layer_index, scalar_refs, history_refs, q_wide, total):
    user_ref, offset_ref, length_ref = scalar_refs
    spot_masks, member_masks, spot_of_chip, row_count = masks
    spots = len(spot_masks)
    dim = total.shape[1]
    scale = 0.5 / math.sqrt(dim)
    chip, _, _ = position(spot_bits)
    spot_part = chip & spot_of_chip
    member_part = chip - spot_part

    def visit(ref, first, count, member, at):
        keys, values = [], []
        for piece in range(count):
            for block in range(ref.shape[2] // BLOCK):
                source = (member | (spot_part ^ spot_masks[at + piece])) * (ref.shape[2] // BLOCK) + block
                owner = user_ref[source]
                limit = length_ref[owner] - offset_ref[source] * BLOCK
                lanes = lax.broadcasted_iota(jnp.int32, (BLOCK, LANES), 1)
                sublanes = lax.broadcasted_iota(jnp.int32, (BLOCK, LANES), 0)
                seen = (lanes == owner) & (sublanes < limit)
                side = jnp.where(seen, 0.0, FAR).astype(jnp.bfloat16)
                at_rows = pl.ds(block * BLOCK, BLOCK)
                keys.append(jnp.concatenate([ref[first + piece, 0, at_rows], side], axis=1))
                values.append(ref[first + piece, 1, at_rows])
        half = lax.dot_general(
            q_wide[...],
            jnp.concatenate(keys, axis=0),
            (((1,), (1,)), ((), ())),
            preferred_element_type=jnp.float32,
        )
        weights = half_silu(half * scale).astype(jnp.bfloat16)
        total[...] += jnp.dot(
            weights, jnp.concatenate(values, axis=0), preferred_element_type=jnp.float32
        )

    if len(history_refs) == len(held):
        for ref, (mask, at) in zip(history_refs, held):
            visit(ref, 0, ref.shape[0], member_part ^ mask, at)
    else:

        @pl.loop(0, len(member_masks))
        def _(turn):
            member = turn * 0
            for i in range((len(member_masks) - 1).bit_length()):
                member = member | (((turn >> i) & 1) * member_masks[1 << i])
            visit(history_refs[0], turn * spots, spots, member, 0)


def attend_kernel(spot_bits, masks, held, layer_index, *refs):
    user_ref, offset_ref, length_ref, count_ref, q_ref, own_ref = refs[:6]
    history_refs, (q_wide, total) = refs[6:-2], refs[-2:]
    spot_masks, member_masks, spot_of_chip, row_count = masks
    spots = len(spot_masks)
    rows = q_ref.shape[0] // spots
    dim = q_ref.shape[1]
    user_count = length_ref.shape[0]
    chip, _, _ = position(spot_bits)
    member_part = chip - (chip & spot_of_chip)
    lane = lax.broadcasted_iota(jnp.int32, (1, LANES), 1)
    starts = jnp.zeros((1, LANES), jnp.int32)
    ends = jnp.zeros((1, LANES), jnp.int32)
    running = jnp.int32(0)
    for user in range(user_count):
        starts = jnp.where(lane == user, running, starts)
        running = running + count_ref[user]
        ends = jnp.where(lane == user, running, ends)
    q_wide[:, :dim] = q_ref[...]
    for at in range(spots):
        first = (member_part | spot_masks[at]) * row_count
        index = first + lax.broadcasted_iota(jnp.int32, (rows, LANES), 0)
        mine = (index >= starts) & (index < ends)
        q_wide[at * rows : (at + 1) * rows, dim:] = jnp.where(mine, 1.0, 0.0).astype(
            jnp.bfloat16
        )
    total[...] = own_ref[...]
    visit_history(
        spot_bits,
        masks,
        held,
        layer_index,
        (user_ref, offset_ref, length_ref),
        history_refs,
        q_wide,
        total,
    )


def finish_kernel(spot_bits, masks, held, layer_index, last, *refs):
    scalar_refs, (q_wide, before_ref, gate_ref), refs = refs[:3], refs[3:6], refs[6:]
    spots = len(masks[0])
    outs = spots if last else 1
    history_refs, o_refs, total = refs[: -outs - 1], refs[-outs - 1 : -1], refs[-1]
    rows = before_ref.shape[0] // spots
    _, spot, _ = position(spot_bits)
    total[...] = before_ref[...]
    if history_refs:
        visit_history(
            spot_bits, masks, held, layer_index, scalar_refs, history_refs, q_wide, total
        )
    full = total[...]
    centred = full - jnp.mean(full, axis=-1, keepdims=True)
    variance = jnp.mean(centred * centred, axis=-1, keepdims=True)
    gated = centred * lax.rsqrt(variance + 1e-05) * gate_ref[...].astype(jnp.float32)
    if not last:
        o_refs[0][...] = gated.astype(jnp.bfloat16)
        return
    total[...] = gated
    for step in range(spots):
        at_rows = pl.ds(pl.multiple_of((spot ^ step) * rows, rows), rows)
        o_refs[step][...] = total[at_rows].astype(jnp.bfloat16)


def body(
    candidate_rows,
    weight_in,
    weight_out,
    history_cache,
    block_user,
    block_offset,
    history_length,
    candidate_count,
):
    own_rows, model_width = candidate_rows.shape
    layers, model_again, heads_here, packed = weight_in.shape
    head_dim = packed // 4
    local_rows = history_cache.shape[2]
    cores = lax.axis_size("cand")
    chips = lax.axis_size("users")
    spots = heads_here
    groups = chips // spots
    row_count = own_rows * cores
    all_rows = row_count * spots
    score_scale = 1.0 / math.sqrt(head_dim)

    bits = list(range(chips.bit_length() - 1))
    spot_bits = sorted((bits[::2] + bits[1::2])[: spots.bit_length() - 1])
    member_bits = [b for b in bits if b not in spot_bits]

    def mask_of(number, places):
        return sum(((number >> i) & 1) << b for i, b in enumerate(places))

    def swap(value, mask):
        return lax.ppermute(value, "users", [(u, u ^ mask) for u in range(chips)])

    def trade_spots(values, diagonal_first=True):
        steps = range(1, spots)
        moved = {0: values[0]}
        for m in reversed(steps) if diagonal_first else steps:
            moved[m] = swap(values[m], mask_of(m, spot_bits))
        return [moved[m] for m in range(spots)]

    def gather_spots(value):
        found = [value]
        for bit in reversed(range(len(spot_bits))):
            mask = 1 << spot_bits[bit]
            found = [(v, swap(v, mask)) for v in found]
            found = [v for v, _ in found] + [w for _, w in found]
        order = [0]
        for bit in reversed(range(len(spot_bits))):
            order = order + [o | (1 << bit) for o in order]
        return [found[order.index(m)] for m in range(spots)]

    def shift_core(value, step):
        pairs = [(c, (c + step) % cores) for c in range(cores)]
        return lax.ppermute(value, "cand", pairs)

    spot_masks = [mask_of(m, spot_bits) for m in range(spots)]
    member_masks = [mask_of(m, member_bits) for m in range(groups)]

    masks = (spot_masks, member_masks, spot_masks[-1], row_count)

    def gather_members(pieces):
        if groups <= 2:
            return [pieces] + [swap(pieces, mask) for mask in member_masks[1:]]
        chips_of = [[mask_of(s, spot_bits) | m for m in member_masks] for s in range(spots)]
        return [
            lax.all_gather(pieces, "users", axis=0, axis_index_groups=chips_of, tiled=True)
        ]

    def after(value, *others):
        return lax.optimization_barrier((value,) + others)[0]

    def kernel_call(kernel, outs, name, operands, scratch=(), limit=8, specs=None):
        results = pl.pallas_call(
            kernel,
            out_shape=[jax.ShapeDtypeStruct(*out) for out in outs],
            in_specs=specs or [VMEM_SPEC] * len(operands),
            out_specs=[VMEM_SPEC] * len(outs),
            scratch_shapes=scratch,
            compiler_params=pltpu.CompilerParams(vmem_limit_bytes=limit * MIB),
            name=name,
        )(*operands)
        return list(results)

    def pick_head(layer_index):
        rows = min(model_width, 128)
        chunks = model_width // rows
        return kernel_call(
            functools.partial(pick_head_kernel, layer_index, spot_bits),
            [((model_width, packed), weight_in.dtype)],
            "pick_head",
            [weight_in],
            [
                pltpu.VMEM((chunks, rows, heads_here, packed), weight_in.dtype),
                pltpu.SemaphoreType.DMA((chunks,)),
            ],
            51,
            [pl.BlockSpec(memory_space=pl.ANY)],
        )[0]

    def order_history():
        shape = (layers, 2, local_rows, head_dim)
        return kernel_call(
            functools.partial(order_history_kernel, spot_bits),
            [(shape, jnp.bfloat16)] * spots,
            "order_history",
            [history_cache],
            [pltpu.VMEM((spots,) + shape, jnp.bfloat16)],
            4,
        )

    def join_layers(pieces):
        shape = (spots, 2, local_rows, head_dim)
        first, *later = kernel_call(
            functools.partial(join_layers_kernel, spots),
            [(shape, jnp.bfloat16)] * layers,
            "join_layers",
            list(pieces),
        )
        return first, later

    def halves(pieces):
        shape = (pieces.shape[0] // 2,) + pieces.shape[1:]
        return kernel_call(halves_kernel, [(shape, pieces.dtype)] * 2, "halves", [pieces])

    def join(pieces):
        if len(pieces) == 1:
            return pieces[0][None]
        shape = (len(pieces),) + pieces[0].shape
        return kernel_call(join_kernel, [(shape, pieces[0].dtype)], "join", list(pieces))[0]

    def together(*values):
        return lax.optimization_barrier(values)

    sibling_rows = [shift_core(candidate_rows, s) for s in range(1, cores)]
    pieces, first_weight, sibling_rows = together(
        trade_spots(order_history()), pick_head(0), sibling_rows
    )
    first, later = join_layers(pieces)
    x_pieces = trade_spots([after(candidate_rows, first)] * spots)
    crossed = groups == 4
    if crossed:
        near_mask, far_mask = member_masks[1:3]
        far = swap(first, far_mask)
        near = swap(first, near_mask)
        far, near = together(far, near)
        onward = swap(far, near_mask)
        x_pieces[1:] = [after(piece, far) for piece in x_pieces[1:]]
        history = [[first, near, far, onward]]
    else:
        history = [gather_members(first)]
    x_group = list(x_pieces)
    for s in range(1, cores):
        x_group += [sibling_rows[s - 1]] + [shift_core(piece, s) for piece in x_pieces[1:]]

    scalars = [block_user, block_offset, history_length, candidate_count]
    one_head = (all_rows, head_dim)
    head_outs = [(one_head, jnp.bfloat16), (one_head, jnp.bfloat16), (one_head, jnp.float32)]
    x, *projected = kernel_call(
        functools.partial(begin_kernel, spots, cores, spot_bits, score_scale),
        [((all_rows, model_width), jnp.bfloat16)] + head_outs,
        "begin",
        x_group + [first_weight],
    )

    for layer_index in range(layers):
        last = layer_index + 1 == layers
        outs = [((row_count, head_dim), jnp.bfloat16)] * spots if last else head_outs[:1]
        query, gate, own = projected
        held, split = (), 1
        if crossed:
            parts = 2 if layer_index else 1
            cuts = [spots // parts * part for part in range(parts)]
            held = ((0, 0), (near_mask, 0))
            held += tuple((m, at) for m in (far_mask, near_mask | far_mask) for at in cuts)
            split = 2 + parts + parts // 2
        ready, coming = history[layer_index][:split], history[layer_index][split:]
        operands = scalars + [query, own] + ready
        wide_query, total = kernel_call(
            functools.partial(attend_kernel, spot_bits, masks, held[:split], layer_index),
            [((all_rows, head_dim + LANES), jnp.bfloat16), (one_head, jnp.float32)],
            "attend",
            operands,
            (),
            16,
            [SMEM_SPEC] * 4 + [VMEM_SPEC] * (len(operands) - 4),
        )
        operands = scalars[:3] + [wide_query, total, gate] + coming
        gated = kernel_call(
            functools.partial(finish_kernel, spot_bits, masks, held[split:], layer_index, last),
            outs,
            "finish",
            operands,
            [pltpu.VMEM(one_head, jnp.float32)],
            16,
            [SMEM_SPEC] * 3 + [VMEM_SPEC] * (len(operands) - 3),
        )
        if not last:
            gated = trade_spots(list(gated) * spots, False)
            next_weight = pick_head(layer_index + 1)
            if crossed:
                whole = after(later[layer_index], far, near)
                far, near = swap(whole, far_mask), swap(whole, near_mask)
                far = halves(after(far, near, gated[1]))
                ahead = swap(far[0], near_mask)
                early, far, next_weight = together(gated[:-1], far, next_weight)
                parts = [(0, early), (spots - 1, gated[-1:])]
            else:
                arrays = gather_members(later[layer_index])
                parts = [(0, gated)]
            terms = []
            for first_step, heads in parts:
                terms = kernel_call(
                    functools.partial(term_kernel, spot_bits, layer_index, first_step),
                    [
                        (
                            (all_rows, model_width),
                            jnp.bfloat16 if first_step + len(heads) == spots else jnp.float32,
                        )
                    ],
                    "term",
                    heads + [weight_out] + terms,
                )
            if crossed:
                terms, ahead = together(terms, ahead)
                arrays = [whole, near] + far + [ahead, swap(far[1], near_mask)]
            terms = terms + [shift_core(terms[0], s) for s in range(1, cores)]
            history.append(arrays)
            x, *projected = kernel_call(
                functools.partial(step_kernel, spots, cores, spot_bits, score_scale),
                [((own_rows, model_width), jnp.bfloat16)] + head_outs,
                "step",
                terms + [x, next_weight],
                [pltpu.VMEM((all_rows, model_width), jnp.bfloat16)],
                12,
            )
        else:
            terms = kernel_call(
                functools.partial(last_term_kernel, spots, cores, spot_bits, layer_index),
                [((own_rows, model_width), jnp.bfloat16)] * cores,
                "last_term",
                trade_spots(gated) + [weight_out],
                [
                    pltpu.VMEM((row_count, spots * head_dim), jnp.bfloat16),
                    pltpu.VMEM((row_count, model_width), jnp.float32),
                ],
            )
            terms = terms[:1] + [shift_core(terms[s], s) for s in range(1, cores)]
            (out,) = kernel_call(
                add_kernel, [((own_rows, model_width), jnp.bfloat16)], "add", [x] + terms
            )
    return out


def solution(mesh):
    placed = (
        P(("users", "cand"), None),
        P(None, None, "cand", None),
        P(None, "cand", None, None),
        P(None, None, "users", "cand", None),
        P(),
        P(),
        P(),
        P(),
    )
    return jax.shard_map(
        body, mesh=mesh, in_specs=placed, out_specs=P(("users", "cand"), None), check_vma=False
    )
```

```python
import functools
import math

import jax
import jax.numpy as jnp
from jax import lax
from jax.experimental import pallas as pl
from jax.experimental.pallas import tpu as pltpu
from jax.sharding import PartitionSpec as P

BLOCK = 128
LANES = 128
FAR = -1e30
MIB = 1024 * 1024

VMEM_SPEC = pl.BlockSpec(memory_space=pltpu.VMEM)
SMEM_SPEC = pl.BlockSpec(memory_space=pltpu.SMEM)


def half_silu(half):
    return half + half * jnp.tanh(half)


def position(spot_bits):
    chip = lax.axis_index("users")
    spot = sum((((chip >> b) & 1) << i for i, b in enumerate(spot_bits)), chip * 0)
    return chip, spot, lax.axis_index("cand")


def order_history_kernel(spot_bits, h_ref, *refs):
    o_refs, pieces = refs[:-1], refs[-1]
    _, spot, _ = position(spot_bits)
    for layer_index in range(h_ref.shape[0]):
        for kind in range(h_ref.shape[1]):
            by_head = jnp.swapaxes(h_ref[layer_index, kind], 0, 1)
            for head in range(h_ref.shape[3]):
                pieces[spot ^ head, layer_index, kind] = by_head[head]
    for step, o_ref in enumerate(o_refs):
        o_ref[...] = pieces[step]


def join_layers_kernel(count, *refs):
    for layer_index, o_ref in enumerate(refs[count:]):
        for at, ref in enumerate(refs[:count]):
            o_ref[at] = ref[layer_index]


def halves_kernel(i_ref, low_ref, high_ref):
    size = low_ref.shape[0]
    low_ref[...] = i_ref[:size]
    high_ref[...] = i_ref[size:]


def join_kernel(*refs):
    o_ref = refs[-1]
    for at, ref in enumerate(refs[:-1]):
        o_ref[at] = ref[...]


def pick_head_kernel(layer_index, spot_bits, w_ref, o_ref, held, sems):
    _, spot, _ = position(spot_bits)
    chunks, rows = held.shape[:2]
    copies = [
        pltpu.make_async_copy(
            w_ref.at[layer_index, pl.ds(at * rows, rows)], held.at[at], sems.at[at]
        )
        for at in range(chunks)
    ]
    for copy in copies:
        copy.start()
    for at, copy in enumerate(copies):
        copy.wait()
        by_head = jnp.swapaxes(held[at], 0, 1)
        for head in range(held.shape[2]):

            @pl.when(spot == head)
            def _(at=at, head=head, by_head=by_head):
                o_ref[at * rows : (at + 1) * rows] = by_head[head]


def project(x_ref, w_ref, q_ref, gate_ref, own_ref, score_scale):
    dim = q_ref.shape[1]

    def part(first):
        w = w_ref[:, first * dim : (first + 2) * dim]
        mixed = jnp.dot(x_ref[...], w, preferred_element_type=jnp.float32)
        return half_silu(mixed * 0.5).astype(jnp.bfloat16)

    tail = part(2)
    query = tail[:, :dim]
    q_ref[...] = query
    score = jnp.sum(
        query.astype(jnp.float32) * tail[:, dim:].astype(jnp.float32), axis=-1, keepdims=True
    )
    weight = half_silu(score * (0.5 * score_scale)).astype(jnp.bfloat16).astype(jnp.float32)
    front = part(0)
    gate_ref[...] = front[:, :dim]
    own_ref[...] = weight * front[:, dim:].astype(jnp.float32)


def begin_kernel(spots, cores, spot_bits, score_scale, *refs):
    _, spot, core_here = position(spot_bits)
    x_refs, (w_ref, x_out, q_ref, gate_ref, own_ref) = refs[:-5], refs[-5:]
    own_rows = x_out.shape[0] // (spots * cores)
    for shift in range(cores):
        core = lax.rem(core_here + (cores - shift), cores)
        for step in range(spots):
            piece = x_refs[shift * spots + step][...]
            at = ((spot ^ step) * cores + core) * own_rows
            x_out[pl.ds(pl.multiple_of(at, own_rows), own_rows)] = piece
    project(x_out, w_ref, q_ref, gate_ref, own_ref, score_scale)


def gather_heads(gated_refs, spot, wide):
    dim = gated_refs[0].shape[1]
    for step, ref in enumerate(gated_refs):
        at = pl.multiple_of((spot ^ step) * dim, dim)
        wide[:, pl.ds(at, dim)] = ref[...]


def term_kernel(spot_bits, layer_index, first_step, *refs):
    _, spot, _ = position(spot_bits)
    count = len(refs) - 2 - (1 if first_step else 0)
    gated_refs, (weight_ref, *before_refs, o_ref) = refs[:count], refs[count:]
    gated = jnp.concatenate([ref[...] for ref in gated_refs], axis=1)
    width = o_ref.shape[1]
    tile = min(width, 256)
    for first in range(0, width, tile):
        columns = slice(first, first + tile)
        weight = jnp.concatenate(
            [weight_ref[layer_index, spot ^ (first_step + at), :, columns] for at in range(count)],
            axis=0,
        )
        term = jnp.dot(gated, weight, preferred_element_type=jnp.float32)
        if before_refs:
            term = term + before_refs[0][:, columns]
        o_ref[:, columns] = term.astype(o_ref.dtype)


def step_kernel(spots, cores, spot_bits, score_scale, *refs):
    _, spot, core = position(spot_bits)
    term_refs, (x_ref, w_ref, x_own, q_ref, gate_ref, own_ref, x_next) = refs[:cores], refs[cores:]
    total = x_ref[...].astype(jnp.float32)
    for ref in term_refs:
        total = total + ref[...].astype(jnp.float32)
    x_next[...] = total.astype(jnp.bfloat16)
    own_rows = x_own.shape[0]
    at = (spot * cores + core) * own_rows
    x_own[...] = x_next[pl.ds(pl.multiple_of(at, own_rows), own_rows)]
    project(x_next, w_ref, q_ref, gate_ref, own_ref, score_scale)


def last_term_kernel(spots, cores, spot_bits, layer_index, *refs):
    _, spot, core = position(spot_bits)
    gated_refs, (weight_ref, *o_refs, wide, total) = refs[:spots], refs[spots:]
    gather_heads(gated_refs, spot, wide)
    own_rows, width = o_refs[0].shape
    weight = weight_ref[layer_index].reshape(wide.shape[1], width)
    total[...] = jnp.dot(wide[...], weight, preferred_element_type=jnp.float32)
    for shift, o_ref in enumerate(o_refs):
        at = lax.rem(core + shift, cores) * own_rows
        o_ref[...] = total[pl.ds(pl.multiple_of(at, own_rows), own_rows)].astype(jnp.bfloat16)


def add_kernel(*refs):
    total = refs[0][...].astype(jnp.float32)
    for ref in refs[1:-1]:
        total = total + ref[...].astype(jnp.float32)
    refs[-1][...] = total.astype(jnp.bfloat16)


def visit_history(spot_bits, masks, held, layer_index, scalar_refs, history_refs, q_wide, total):
    user_ref, offset_ref, length_ref = scalar_refs
    spot_masks, member_masks, spot_of_chip, row_count = masks
    spots = len(spot_masks)
    dim = total.shape[1]
    scale = 0.5 / math.sqrt(dim)
    chip, _, _ = position(spot_bits)
    spot_part = chip & spot_of_chip
    member_part = chip - spot_part

    def visit(ref, first, count, member, at):
        keys, values = [], []
        for piece in range(count):
            for block in range(ref.shape[2] // BLOCK):
                source = (member | (spot_part ^ spot_masks[at + piece])) * (ref.shape[2] // BLOCK) + block
                owner = user_ref[source]
                limit = length_ref[owner] - offset_ref[source] * BLOCK
                lanes = lax.broadcasted_iota(jnp.int32, (BLOCK, LANES), 1)
                sublanes = lax.broadcasted_iota(jnp.int32, (BLOCK, LANES), 0)
                seen = (lanes == owner) & (sublanes < limit)
                side = jnp.where(seen, 0.0, FAR).astype(jnp.bfloat16)
                at_rows = pl.ds(block * BLOCK, BLOCK)
                keys.append(jnp.concatenate([ref[first + piece, 0, at_rows], side], axis=1))
                values.append(ref[first + piece, 1, at_rows])
        half = lax.dot_general(
            q_wide[...],
            jnp.concatenate(keys, axis=0),
            (((1,), (1,)), ((), ())),
            preferred_element_type=jnp.float32,
        )
        weights = half_silu(half * scale).astype(jnp.bfloat16)
        total[...] += jnp.dot(
            weights, jnp.concatenate(values, axis=0), preferred_element_type=jnp.float32
        )

    if len(history_refs) == len(held):
        for ref, (mask, at) in zip(history_refs, held):
            visit(ref, 0, ref.shape[0], member_part ^ mask, at)
    else:

        @pl.loop(0, len(member_masks))
        def _(turn):
            member = turn * 0
            for i in range((len(member_masks) - 1).bit_length()):
                member = member | (((turn >> i) & 1) * member_masks[1 << i])
            visit(history_refs[0], turn * spots, spots, member, 0)


def attend_kernel(spot_bits, masks, held, layer_index, *refs):
    user_ref, offset_ref, length_ref, count_ref, q_ref, own_ref = refs[:6]
    history_refs, (q_wide, total) = refs[6:-2], refs[-2:]
    spot_masks, member_masks, spot_of_chip, row_count = masks
    spots = len(spot_masks)
    rows = q_ref.shape[0] // spots
    dim = q_ref.shape[1]
    user_count = length_ref.shape[0]
    chip, _, _ = position(spot_bits)
    member_part = chip - (chip & spot_of_chip)
    lane = lax.broadcasted_iota(jnp.int32, (1, LANES), 1)
    starts = jnp.zeros((1, LANES), jnp.int32)
    ends = jnp.zeros((1, LANES), jnp.int32)
    running = jnp.int32(0)
    for user in range(user_count):
        starts = jnp.where(lane == user, running, starts)
        running = running + count_ref[user]
        ends = jnp.where(lane == user, running, ends)
    q_wide[:, :dim] = q_ref[...]
    for at in range(spots):
        first = (member_part | spot_masks[at]) * row_count
        index = first + lax.broadcasted_iota(jnp.int32, (rows, LANES), 0)
        mine = (index >= starts) & (index < ends)
        q_wide[at * rows : (at + 1) * rows, dim:] = jnp.where(mine, 1.0, 0.0).astype(
            jnp.bfloat16
        )
    total[...] = own_ref[...]
    visit_history(
        spot_bits,
        masks,
        held,
        layer_index,
        (user_ref, offset_ref, length_ref),
        history_refs,
        q_wide,
        total,
    )


def finish_kernel(spot_bits, masks, held, layer_index, last, *refs):
    scalar_refs, (q_wide, before_ref, gate_ref), refs = refs[:3], refs[3:6], refs[6:]
    spots = len(masks[0])
    outs = spots if last else 1
    history_refs, o_refs, total = refs[: -outs - 1], refs[-outs - 1 : -1], refs[-1]
    rows = before_ref.shape[0] // spots
    _, spot, _ = position(spot_bits)
    total[...] = before_ref[...]
    if history_refs:
        visit_history(
            spot_bits, masks, held, layer_index, scalar_refs, history_refs, q_wide, total
        )
    full = total[...]
    centred = full - jnp.mean(full, axis=-1, keepdims=True)
    variance = jnp.mean(centred * centred, axis=-1, keepdims=True)
    gated = centred * lax.rsqrt(variance + 1e-05) * gate_ref[...].astype(jnp.float32)
    if not last:
        o_refs[0][...] = gated.astype(jnp.bfloat16)
        return
    total[...] = gated
    for step in range(spots):
        at_rows = pl.ds(pl.multiple_of((spot ^ step) * rows, rows), rows)
        o_refs[step][...] = total[at_rows].astype(jnp.bfloat16)


def body(
    candidate_rows,
    weight_in,
    weight_out,
    history_cache,
    block_user,
    block_offset,
    history_length,
    candidate_count,
):
    own_rows, model_width = candidate_rows.shape
    layers, model_again, heads_here, packed = weight_in.shape
    head_dim = packed // 4
    local_rows = history_cache.shape[2]
    cores = lax.axis_size("cand")
    chips = lax.axis_size("users")
    spots = heads_here
    groups = chips // spots
    row_count = own_rows * cores
    all_rows = row_count * spots
    score_scale = 1.0 / math.sqrt(head_dim)

    bits = list(range(chips.bit_length() - 1))
    spot_bits = sorted((bits[::2] + bits[1::2])[: spots.bit_length() - 1])
    member_bits = [b for b in bits if b not in spot_bits]

    def mask_of(number, places):
        return sum(((number >> i) & 1) << b for i, b in enumerate(places))

    def swap(value, mask):
        return lax.ppermute(value, "users", [(u, u ^ mask) for u in range(chips)])

    def trade_spots(values, diagonal_first=True):
        steps = range(1, spots)
        moved = {0: values[0]}
        for m in reversed(steps) if diagonal_first else steps:
            moved[m] = swap(values[m], mask_of(m, spot_bits))
        return [moved[m] for m in range(spots)]

    def gather_spots(value):
        found = [value]
        for bit in reversed(range(len(spot_bits))):
            mask = 1 << spot_bits[bit]
            found = [(v, swap(v, mask)) for v in found]
            found = [v for v, _ in found] + [w for _, w in found]
        order = [0]
        for bit in reversed(range(len(spot_bits))):
            order = order + [o | (1 << bit) for o in order]
        return [found[order.index(m)] for m in range(spots)]

    def shift_core(value, step):
        pairs = [(c, (c + step) % cores) for c in range(cores)]
        return lax.ppermute(value, "cand", pairs)

    spot_masks = [mask_of(m, spot_bits) for m in range(spots)]
    member_masks = [mask_of(m, member_bits) for m in range(groups)]

    masks = (spot_masks, member_masks, spot_masks[-1], row_count)

    def gather_members(pieces):
        if groups <= 2:
            return [pieces] + [swap(pieces, mask) for mask in member_masks[1:]]
        chips_of = [[mask_of(s, spot_bits) | m for m in member_masks] for s in range(spots)]
        return [
            lax.all_gather(pieces, "users", axis=0, axis_index_groups=chips_of, tiled=True)
        ]

    def after(value, *others):
        return lax.optimization_barrier((value,) + others)[0]

    def kernel_call(kernel, outs, name, operands, scratch=(), limit=8, specs=None):
        results = pl.pallas_call(
            kernel,
            out_shape=[jax.ShapeDtypeStruct(*out) for out in outs],
            in_specs=specs or [VMEM_SPEC] * len(operands),
            out_specs=[VMEM_SPEC] * len(outs),
            scratch_shapes=scratch,
            compiler_params=pltpu.CompilerParams(vmem_limit_bytes=limit * MIB),
            name=name,
        )(*operands)
        return list(results)

    def pick_head(layer_index):
        rows = min(model_width, 128)
        chunks = model_width // rows
        return kernel_call(
            functools.partial(pick_head_kernel, layer_index, spot_bits),
            [((model_width, packed), weight_in.dtype)],
            "pick_head",
            [weight_in],
            [
                pltpu.VMEM((chunks, rows, heads_here, packed), weight_in.dtype),
                pltpu.SemaphoreType.DMA((chunks,)),
            ],
            51,
            [pl.BlockSpec(memory_space=pl.ANY)],
        )[0]

    def order_history():
        shape = (layers, 2, local_rows, head_dim)
        return kernel_call(
            functools.partial(order_history_kernel, spot_bits),
            [(shape, jnp.bfloat16)] * spots,
            "order_history",
            [history_cache],
            [pltpu.VMEM((spots,) + shape, jnp.bfloat16)],
            4,
        )

    def join_layers(pieces):
        shape = (spots, 2, local_rows, head_dim)
        first, *later = kernel_call(
            functools.partial(join_layers_kernel, spots),
            [(shape, jnp.bfloat16)] * layers,
            "join_layers",
            list(pieces),
        )
        return first, later

    def halves(pieces):
        shape = (pieces.shape[0] // 2,) + pieces.shape[1:]
        return kernel_call(halves_kernel, [(shape, pieces.dtype)] * 2, "halves", [pieces])

    def join(pieces):
        if len(pieces) == 1:
            return pieces[0][None]
        shape = (len(pieces),) + pieces[0].shape
        return kernel_call(join_kernel, [(shape, pieces[0].dtype)], "join", list(pieces))[0]

    def together(*values):
        return lax.optimization_barrier(values)

    sibling_rows = [shift_core(candidate_rows, s) for s in range(1, cores)]
    pieces, first_weight, sibling_rows = together(
        trade_spots(order_history()), pick_head(0), sibling_rows
    )
    first, later = join_layers(pieces)
    x_pieces = trade_spots([after(candidate_rows, first)] * spots)
    crossed = groups == 4
    if crossed:
        near_mask, far_mask = member_masks[1:3]
        far = swap(first, far_mask)
        near = swap(first, near_mask)
        far, near = together(far, near)
        onward = swap(far, near_mask)
        x_pieces[1:] = [after(piece, far) for piece in x_pieces[1:]]
        history = [[first, near, far, onward]]
    else:
        history = [gather_members(first)]
    x_group = list(x_pieces)
    for s in range(1, cores):
        x_group += [sibling_rows[s - 1]] + [shift_core(piece, s) for piece in x_pieces[1:]]

    scalars = [block_user, block_offset, history_length, candidate_count]
    one_head = (all_rows, head_dim)
    head_outs = [(one_head, jnp.bfloat16), (one_head, jnp.bfloat16), (one_head, jnp.float32)]
    x, *projected = kernel_call(
        functools.partial(begin_kernel, spots, cores, spot_bits, score_scale),
        [((all_rows, model_width), jnp.bfloat16)] + head_outs,
        "begin",
        x_group + [first_weight],
    )

    for layer_index in range(layers):
        last = layer_index + 1 == layers
        outs = [((row_count, head_dim), jnp.bfloat16)] * spots if last else head_outs[:1]
        query, gate, own = projected
        held, split = (), 1
        if crossed:
            parts = 2 if layer_index else 1
            cuts = [spots // parts * part for part in range(parts)]
            held = ((0, 0), (near_mask, 0))
            held += tuple((m, at) for m in (far_mask, near_mask | far_mask) for at in cuts)
            split = 2 + parts + parts // 2
        ready, coming = history[layer_index][:split], history[layer_index][split:]
        operands = scalars + [query, own] + ready
        wide_query, total = kernel_call(
            functools.partial(attend_kernel, spot_bits, masks, held[:split], layer_index),
            [((all_rows, head_dim + LANES), jnp.bfloat16), (one_head, jnp.float32)],
            "attend",
            operands,
            (),
            16,
            [SMEM_SPEC] * 4 + [VMEM_SPEC] * (len(operands) - 4),
        )
        operands = scalars[:3] + [wide_query, total, gate] + coming
        gated = kernel_call(
            functools.partial(finish_kernel, spot_bits, masks, held[split:], layer_index, last),
            outs,
            "finish",
            operands,
            [pltpu.VMEM(one_head, jnp.float32)],
            16,
            [SMEM_SPEC] * 3 + [VMEM_SPEC] * (len(operands) - 3),
        )
        if not last:
            gated = trade_spots(list(gated) * spots)
            next_weight = pick_head(layer_index + 1)
            if crossed:
                whole = after(later[layer_index], far, near)
                far, near = swap(whole, far_mask), swap(whole, near_mask)
                far = halves(after(far, near, gated[1]))
                ahead = swap(far[0], near_mask)
                early, far, next_weight = together(gated[:-1], far, next_weight)
                late, ahead = together(gated[-1:], ahead)
                parts = [(0, early), (spots - 1, late)]
                arrays = [whole, near] + far + [ahead, swap(far[1], near_mask)]
            else:
                arrays = gather_members(later[layer_index])
                parts = [(0, gated)]
            terms = []
            for first_step, heads in parts:
                terms = kernel_call(
                    functools.partial(term_kernel, spot_bits, layer_index, first_step),
                    [
                        (
                            (all_rows, model_width),
                            jnp.bfloat16 if first_step + len(heads) == spots else jnp.float32,
                        )
                    ],
                    "term",
                    heads + [weight_out] + terms,
                )
            terms = terms + [shift_core(terms[0], s) for s in range(1, cores)]
            history.append(arrays)
            x, *projected = kernel_call(
                functools.partial(step_kernel, spots, cores, spot_bits, score_scale),
                [((own_rows, model_width), jnp.bfloat16)] + head_outs,
                "step",
                terms + [x, next_weight],
                [pltpu.VMEM((all_rows, model_width), jnp.bfloat16)],
                12,
            )
        else:
            terms = kernel_call(
                functools.partial(last_term_kernel, spots, cores, spot_bits, layer_index),
                [((own_rows, model_width), jnp.bfloat16)] * cores,
                "last_term",
                trade_spots(gated) + [weight_out],
                [
                    pltpu.VMEM((row_count, spots * head_dim), jnp.bfloat16),
                    pltpu.VMEM((row_count, model_width), jnp.float32),
                ],
            )
            terms = terms[:1] + [shift_core(terms[s], s) for s in range(1, cores)]
            (out,) = kernel_call(
                add_kernel, [((own_rows, model_width), jnp.bfloat16)], "add", [x] + terms
            )
    return out


def solution(mesh):
    placed = (
        P(("users", "cand"), None),
        P(None, None, "cand", None),
        P(None, "cand", None, None),
        P(None, None, "users", "cand", None),
        P(),
        P(),
        P(),
        P(),
    )
    return jax.shard_map(
        body, mesh=mesh, in_specs=placed, out_specs=P(("users", "cand"), None), check_vma=False
    )
```
